512 devices in a mesh: row: 16 (over y, core), col: 32 (over z, x).
Axes of the slice: x: 4, y: 8, z: 8, core: 2. Of those that a mesh axis runs over, the one named last changes fastest.
Arguments:
- matrix: float32 [16384, 16384], P('row', 'col'), may hold values from -24 to 24
- panel: float32 [16384, 256], P(('row', 'col')), may hold values from -21 to 21
Outputs:
- updated: float32 [16384, 16384], P('row', 'col')
The draws below stay inside these ranges and needn't reach their ends.
All inputs are finite; a program needn't handle non-finite values.
Results may differ from the reference program's by a relative error of at most 0.0003.
Values sent between devices are 32-bit elements; how exact they have to be, the bound alone decides.
A program may use at most 64 MiB of HBM per device.

```python
import jax
import jax.numpy as jnp
from jax import lax

N = 16384
B = 256


def draw_matrix(key, part):
    key = jax.random.fold_in(key, 11)
    first = jax.random.fold_in(key, 0)
    base = jnp.clip(jax.random.normal(first, (N, N), jnp.float32), -6.0, 6.0)
    sym = 0.5 * (base + base.T)
    return sym


def draw_panel(key, part):
    key = jax.random.fold_in(key, 23)
    first = jax.random.fold_in(key, 0)
    rising = 1.0 + 2.0 * jnp.arange(N, dtype=jnp.float32) / N
    values = jnp.clip(jax.random.normal(first, (N, B), jnp.float32), -6.0, 6.0)
    return values * rising[:, None]


def setup_inputs(seed: int = 0) -> dict:
    arg_keys = jax.random.split(jax.random.key(seed), 3)
    return {
        "matrix": draw_matrix(jax.random.fold_in(arg_keys[2], 71), 0),
        "panel": draw_panel(jax.random.fold_in(arg_keys[2], 71), 0),
    }


HIGH = lax.Precision.HIGHEST

def mult(left, right):
    return jnp.dot(left.astype(jnp.float32), right.astype(jnp.float32), precision=HIGH, preferred_element_type=jnp.float32)

def reference(matrix, panel):
    gram = mult(panel.T, panel)
    factor = jnp.linalg.cholesky(gram)
    basis = jax.scipy.linalg.solve_triangular(factor, panel.T, lower=True).T
    product = mult(matrix, basis)
    inner = mult(basis.T, product)
    shifted = product - 0.5 * mult(basis, inner)
    blocks = N // 512
    rows_a = matrix.reshape(blocks, 512, N)
    rows_v = basis.reshape(blocks, 512, B)
    rows_s = shifted.reshape(blocks, 512, B)
    starts = jnp.arange(blocks, dtype=jnp.int32) * 512

    def one_block(items):
        block_a, block_v, block_s, start = items
        change = mult(block_v, shifted.T) + mult(block_s, basis.T)
        row_ids = start + jnp.arange(512, dtype=jnp.int32)
        col_ids = jnp.arange(N, dtype=jnp.int32)
        lower = row_ids[:, None] >= col_ids[None, :]
        return jnp.where(lower, block_a - change, block_a)
    result = lax.map(one_block, (rows_a, rows_v, rows_s, starts))
    return result.reshape(N, N)
```

```python
import functools

import jax
import jax.numpy as jnp
from jax import lax
from jax.experimental import pallas as pl
from jax.experimental.pallas import tpu as pltpu
from jax.sharding import PartitionSpec as P

HIGH = lax.Precision.HIGHEST
MESH = pl.DeviceIdType.MESH
F32 = jnp.float32
NX, NZ, NR, NC = 4, 8, 16, 32
H = 32
B = 256
G16 = 16
P_Z, P_X, P_PERM, P_ROW = 0, 1, 4, 5
Z_RS, Z_PERM, Z_ROW, Z_Z, Z_X = 6, 7, 8, 9, 10
G_Z, G_X, G_ROW = 14, 15, 16
M_Z, M_X, M_ROW = 17, 18, 19
SEMS = 20


def nn(a, b):
    return jnp.dot(a, b, precision=HIGH, preferred_element_type=F32)


def nt(a, b):
    return lax.dot_general(a, b, (((1,), (1,)), ((), ())), precision=HIGH, preferred_element_type=F32)


def tn(a, b):
    return lax.dot_general(a, b, (((0,), (0,)), ((), ())), precision=HIGH, preferred_element_type=F32)


def kernel(a_hbm, p_ref, out_hbm, a_v, at_v, o_v, pr, zr, pc, pct, zc, zpart, zrs, gz, gx, gf, mz, mx, mf, w, blk, sub,
           xc, yc, send, recv, local):
    r = lax.axis_index("row")
    c = lax.axis_index("col")
    z = c // NX
    x = c % NX
    r2, c2 = c % NR, 2 * r + c // NR
    r1, c1 = c // 2, (c % 2) * NR + r
    alone = jnp.logical_and(r2 == r, c2 == c)

    def z_peer(d):
        return (r, lax.rem(z + d, NZ) * NX + x)

    def x_peer(d):
        return (r, z * NX + lax.rem(x + d, NX))

    def row_peer(d):
        return (lax.rem(r + d, NR), c)

    barrier = pltpu.get_barrier_semaphore()

    def greet(peer, count):
        def body(d, carry):
            pl.semaphore_signal(barrier, inc=1, device_id=peer(d), device_id_type=MESH)
            return carry
        lax.fori_loop(1, count, body, 0)

    greet(z_peer, NZ)
    greet(x_peer, NX)
    greet(row_peer, NR)

    @pl.when(jnp.logical_not(alone))
    def _():
        pl.semaphore_signal(barrier, inc=1, device_id=(r2, c2), device_id_type=MESH)
        pl.semaphore_signal(barrier, inc=1, device_id=(r1, c1), device_id_type=MESH)

    a_copy = pltpu.make_async_copy(a_hbm, a_v, local.at[0])
    a_copy.start()
    pl.semaphore_wait(barrier, NZ - 1 + NX - 1 + NR - 1 + jnp.where(alone, 0, 2))

    def fan(src, dst, peer, count, slot):
        def body(d, carry):
            pltpu.make_async_remote_copy(
                src_ref=src(d), dst_ref=dst(d), send_sem=send.at[slot], recv_sem=recv.at[slot],
                device_id=peer(d), device_id_type=MESH).start()
            return carry
        lax.fori_loop(1, count, body, 0)

    def landed(ref, slot):
        pltpu.make_async_copy(ref, ref, recv.at[slot]).wait()

    def left(ref, slot):
        pltpu.make_async_copy(ref, ref, send.at[slot]).wait()

    def fan_x(buf, slot):
        def body(d, carry):
            pltpu.make_async_remote_copy(
                src_ref=buf.at[:, x], dst_ref=buf.at[:, x], send_sem=send.at[slot + d - 1],
                recv_sem=recv.at[slot + d - 1], device_id=x_peer(d), device_id_type=MESH).start()
            return carry
        lax.fori_loop(1, NX, body, 0)

    def perm(src, dst_slot, dst_buf, device, slot):
        @pl.when(alone)
        def _():
            pltpu.make_async_copy(src, dst_slot(dst_buf), recv.at[slot]).start()

        @pl.when(jnp.logical_not(alone))
        def _():
            pltpu.make_async_remote_copy(
                src_ref=src, dst_ref=dst_slot(dst_buf), send_sem=send.at[slot], recv_sem=recv.at[slot],
                device_id=device, device_id_type=MESH).start()

    perm(p_ref, lambda b: b.at[r2], pc, (r2, c2), P_PERM)
    fan(lambda d: p_ref, lambda d: pr.at[z, x], z_peer, NZ, P_Z)
    pr[z, x] = p_ref[...]
    landed(pc.at[r], P_PERM)
    fan(lambda d: pc.at[r], lambda d: pc.at[r], row_peer, NR, P_ROW)

    a_copy.wait()

    def turn(lo, hi):
        def body(i, carry):
            tile = a_v[i].reshape(128, 512)
            at_v[i] = tile.T
            return carry
        lax.fori_loop(lo, hi, body, 0)

    turn(0, 4)
    landed(pr.at[0:NZ - 1, 0], P_Z)
    fan_x(pr, P_X)
    landed(pc.at[0:NR - 1], P_ROW)
    pct[...] = pc[...].reshape(NR * H, B).T

    def mine(cols):
        rows = pct[pl.ds(pl.multiple_of(r * G16, G16), G16), :]
        return nn(rows, cols[...].reshape(NR * H, B))

    gz[z] = mine(pc)
    fan(lambda d: gz.at[z], lambda d: gz.at[z], z_peer, NZ, G_Z)
    turn(4, 8)
    landed(gz.at[0:NZ - 1], G_Z)
    gx[x] = jnp.sum(gz[...], axis=0)
    fan(lambda d: gx.at[x], lambda d: gx.at[x], x_peer, NX, G_X)
    landed(gx.at[0:NX - 1], G_X)
    gf[r] = jnp.sum(gx[...], axis=0)
    fan(lambda d: gf.at[r], lambda d: gf.at[r], row_peer, NR, G_ROW)

    def arrived_x(buf, slot):
        for d in range(1, NX):
            landed(buf.at[:, 0], slot + d - 1)

    arrived_x(pr, P_X)

    def share(i, carry):
        total = jnp.zeros((256, B), F32)
        for k in range(NZ):
            total += nn(at_v[k, pl.ds(pl.multiple_of(i * 256, 256), 256), :], pr[k].reshape(128, B))
        zpart[pl.ds(i * 8, 8)] = total.reshape(8, H, B)
        return carry
    lax.fori_loop(0, 2, share, 0)
    zrs[r] = zpart[r]
    fan(lambda d: zpart.at[lax.rem(r + d, NR)], lambda d: zrs.at[r], row_peer, NR, Z_RS)

    landed(gf.at[0:NR - 1], G_ROW)
    w[...] = gf[...].reshape(B, B)
    lane = lax.broadcasted_iota(jnp.int32, (128, 128), 1)
    subl = lax.broadcasted_iota(jnp.int32, (128, 128), 0)

    def sweep(lo, hi):
        def body(k, a):
            in_col = lane == k
            in_row = subl == k
            col = jnp.sum(jnp.where(in_col, a, 0.0), axis=1, keepdims=True)
            row = jnp.sum(jnp.where(in_row, a, 0.0), axis=0, keepdims=True)
            piv = jnp.sum(jnp.where(lane[0:1] == k, row, 0.0), axis=1, keepdims=True)
            inv = 1.0 / piv
            scaled = row * inv
            other = a - col * scaled
            other = jnp.where(in_col, col * inv, other)
            return jnp.where(in_row, jnp.where(in_col, -inv, scaled), other)
        blk[...] = lax.fori_loop(lo, hi, body, blk[...])

    blk[...] = w[0:128, 0:128]
    sweep(0, 48)

    landed(zrs.at[0:NR - 1], Z_RS)
    zc[r] = jnp.sum(zrs[...], axis=0)
    perm(zc.at[r], lambda b: b.at[c1 // NX, c1 % NX], zr, (r1, c1), Z_PERM)
    fan(lambda d: zc.at[r], lambda d: zc.at[r], row_peer, NR, Z_ROW)
    sweep(48, 72)
    landed(zr.at[z, x], Z_PERM)
    fan(lambda d: zr.at[z, x], lambda d: zr.at[z, x], z_peer, NZ, Z_Z)
    sweep(72, 100)
    landed(zc.at[0:NR - 1], Z_ROW)
    mz[z] = mine(zc)
    fan(lambda d: mz.at[z], lambda d: mz.at[z], z_peer, NZ, M_Z)
    sweep(100, 128)
    landed(zr.at[0:NZ - 1, 0], Z_Z)
    fan_x(zr, Z_X)
    landed(mz.at[0:NZ - 1], M_Z)
    mx[x] = jnp.sum(mz[...], axis=0)
    fan(lambda d: mx.at[x], lambda d: mx.at[x], x_peer, NX, M_X)
    sub[...] = nn(w[128:256, 0:128], -blk[...])
    w[0:128, 0:128] = -blk[...]
    blk[...] = w[128:256, 128:256] - nt(sub[...], w[128:256, 0:128])
    landed(mx.at[0:NX - 1], M_X)
    mf[r] = jnp.sum(mx[...], axis=0)
    fan(lambda d: mf.at[r], lambda d: mf.at[r], row_peer, NR, M_ROW)
    sweep(0, 128)
    low = nn(blk[...], sub[...])
    w[128:256, 128:256] = -blk[...]
    w[128:256, 0:128] = low
    w[0:128, 128:256] = low.T
    w[0:128, 0:128] = w[0:128, 0:128] - tn(sub[...], low)
    yc[...] = nt(w[...], pc[...].reshape(NR * H, B))
    landed(mf.at[0:NR - 1], M_ROW)
    rest = nn(mf[...].reshape(B, B), yc[...])
    xc[...] = nt(w[...], zc[...].reshape(NR * H, B)) - nn(w[...], rest)

    def update(xx, d):
        change = nn(pr[:, xx].reshape(256, B), xc[...]) + nn(zr[:, xx].reshape(256, B), yc[...])
        t = lax.broadcasted_iota(jnp.int32, (256, 512), 0)
        rows = r * 1024 + (t // H) * (H * NX) + xx * H + t % H
        cols = c * 512 + lax.broadcasted_iota(jnp.int32, (256, 512), 1)
        old = a_v[:, xx].reshape(256, 512)
        o_v[:, xx] = jnp.where(rows >= cols, old - change, old).reshape(NZ, H, 512)
        pltpu.make_async_copy(o_v.at[:, xx], out_hbm.at[:, xx], local.at[1 + d]).start()

    update(x, 0)

    def tail(d, carry):
        landed(zr.at[:, 0], Z_X + d - 1)
        update(lax.rem(x - d + NX, NX), d)
        return carry
    lax.fori_loop(1, NX, tail, 0)

    for slot in (P_Z, Z_Z):
        left(pr.at[0:NZ - 1, 0], slot)
    for slot in (P_X, Z_X):
        for d in range(1, NX):
            left(pr.at[:, 0], slot + d - 1)
    for slot in (P_ROW, Z_RS, Z_ROW):
        left(pc.at[0:NR - 1], slot)
    for slot in (G_Z, M_Z):
        left(gz.at[0:NZ - 1], slot)
    for slot in (G_X, M_X):
        left(gx.at[0:NX - 1], slot)
    for slot in (G_ROW, M_ROW):
        left(gf.at[0:NR - 1], slot)

    @pl.when(jnp.logical_not(alone))
    def _():
        left(pc.at[0], P_PERM)
        left(pc.at[0], Z_PERM)

    def close(d, carry):
        xx = lax.rem(x - d + NX, NX)
        pltpu.make_async_copy(o_v.at[:, xx], out_hbm.at[:, xx], local.at[1 + d]).wait()
        return carry
    lax.fori_loop(0, NX, close, 0)


def on_device(matrix, panel):
    vm = lambda *s: pltpu.VMEM(s, F32)
    out = pl.pallas_call(
        kernel,
        out_shape=jax.ShapeDtypeStruct((NZ, NX, H, 512), F32),
        in_specs=[pl.BlockSpec(memory_space=pl.ANY), pl.BlockSpec(memory_space=pltpu.VMEM)],
        out_specs=pl.BlockSpec(memory_space=pl.ANY),
        scratch_shapes=[
            vm(NZ, NX, H, 512), vm(NZ, 512, 128), vm(NZ, NX, H, 512),
            vm(NZ, NX, H, B), vm(NZ, NX, H, B), vm(NR, H, B), vm(B, NR * H), vm(NR, H, B),
            vm(NR, H, B), vm(NR, H, B),
            vm(NZ, G16, B), vm(NX, G16, B), vm(NR, G16, B),
            vm(NZ, G16, B), vm(NX, G16, B), vm(NR, G16, B),
            vm(B, B), vm(128, 128), vm(128, 128), vm(B, 512), vm(B, 512),
            pltpu.SemaphoreType.DMA((SEMS,)), pltpu.SemaphoreType.DMA((SEMS,)), pltpu.SemaphoreType.DMA((5,)),
        ],
        compiler_params=pltpu.CompilerParams(
            collective_id=0, has_side_effects=True, vmem_limit_bytes=48 * 1024 * 1024),
        cost_estimate=pl.CostEstimate(flops=8 * 10**9, bytes_accessed=8 * 2**20, transcendentals=0),
    )(matrix.reshape(NZ, NX, H, 512), panel)
    return out.reshape(1024, 512)


def solution(mesh):
    return jax.shard_map(
        on_device,
        mesh=mesh,
        in_specs=(P("row", "col"), P(("row", "col"), None)),
        out_specs=P("row", "col"),
        check_vma=False,
    )
```

```python
import jax
import jax.numpy as jnp
from jax import lax
from jax.experimental import pallas as pl
from jax.experimental.pallas import tpu as pltpu
from jax.sharding import PartitionSpec as P

HIGH = lax.Precision.HIGHEST
MESH = pl.DeviceIdType.MESH
F32 = jnp.float32
NX, NY, NZ, NR = 4, 8, 8, 16
H = 32
B = 256
G16 = 16
P_Z, P_X, Z_Z, Z_X = 0, 8, 16, 24
P_PERM, P_Y, P_CORE, Z_CORE, Z_Y, Z_PERM, ZC_Y, ZC_CORE = 32, 33, 34, 35, 36, 37, 38, 39
G_SUM, M_SUM = 40, 46
SEMS = 52


def nn(a, b):
    return jnp.dot(a, b, precision=HIGH, preferred_element_type=F32)


def nt(a, b):
    return lax.dot_general(a, b, (((1,), (1,)), ((), ())), precision=HIGH, preferred_element_type=F32)


def tn(a, b):
    return lax.dot_general(a, b, (((0,), (0,)), ((), ())), precision=HIGH, preferred_element_type=F32)


def kernel(a_hbm, p_hbm, out_hbm, a_v, at_v, o_v, pv, pr, zr, pc, pct, zc, zpart, zcb, zs, zyb,
           gpart, gcb, gs, gyb, gzb, gxb, gf, mpart, mcb, ms, myb, mzb, mxb, mf, w, blk, sub, xc, yc, send, recv, local):
    r = lax.axis_index("row")
    c = lax.axis_index("col")
    y = r // 2
    k = r % 2
    z = c // NX
    x = c % NX
    r2, c2 = c % NR, 2 * r + c // NR
    r1, c1 = c // 2, (c % 2) * NR + r
    alone = jnp.logical_and(r2 == r, c2 == c)
    sibling = (2 * y + 1 - k, c)

    def z_peer(d):
        return (r, (z + d) % NZ * NX + x)

    def x_peer(d):
        return (r, z * NX + (x + d) % NX)

    def y_peer(d):
        return ((y + d) % NY * 2 + k, c)

    def send_to(src, dst, device, out_slot, in_slot):
        pltpu.make_async_remote_copy(
            src_ref=src, dst_ref=dst, send_sem=send.at[out_slot], recv_sem=recv.at[in_slot],
            device_id=device, device_id_type=MESH).start()

    def loop(lo, hi, step):
        def body(d, carry):
            step(d)
            return carry
        lax.fori_loop(lo, hi, body, 0)

    def landed(ref, slot):
        pltpu.make_async_copy(ref, ref, recv.at[slot]).wait()

    def left(ref, slot):
        pltpu.make_async_copy(ref, ref, send.at[slot]).wait()

    barrier = pltpu.get_barrier_semaphore()

    def greet(device):
        pl.semaphore_signal(barrier, inc=1, device_id=device, device_id_type=MESH)

    loop(1, NZ, lambda d: greet(z_peer(d)))
    loop(1, NX, lambda d: greet(x_peer(d)))
    loop(1, NY, lambda d: greet(y_peer(d)))
    greet(sibling)

    @pl.when(jnp.logical_not(alone))
    def _():
        greet((r2, c2))
        greet((r1, c1))

    p_copy = pltpu.make_async_copy(p_hbm, pv, local.at[4])
    a_copy = pltpu.make_async_copy(a_hbm, a_v, local.at[0])
    p_copy.start()
    a_copy.start()
    p_copy.wait()
    pr[z, x] = pv[...]
    gpart[...] = tn(pv[...], pv[...]).reshape(NY, 2, G16, B)
    pl.semaphore_wait(barrier, NZ - 1 + NX - 1 + NY - 1 + 1 + jnp.where(alone, 0, 2))

    def perm(src, dst, device, slot):
        @pl.when(alone)
        def _():
            pltpu.make_async_copy(src, dst, recv.at[slot]).start()

        @pl.when(jnp.logical_not(alone))
        def _():
            send_to(src, dst, device, slot, slot)

    def order(j):
        return jnp.where(j % 2 == 0, j // 2 + 1, NZ - 1 - j // 2)

    def gather_start(buf, zslot, xslot):
        loop(0, NZ - 1, lambda j: send_to(buf.at[z, x], buf.at[z, x], z_peer(order(j)), zslot, zslot + order(j)))
        loop(1, NX, lambda e: send_to(buf.at[z, x], buf.at[z, x], x_peer(e), xslot, xslot))

    def gather_forward(buf, zslot, xslot, lo, hi):
        def step(j):
            d = order(j)
            zz = (z - d + NZ) % NZ
            landed(buf.at[zz, x], zslot + d)
            loop(1, NX, lambda e: send_to(buf.at[zz, x], buf.at[zz, x], x_peer(e), xslot, xslot + d))
        loop(lo, hi, step)

    def gather_wait(buf, xslot, g):
        for i in range(2):
            zz = 2 * g + i
            landed(buf.at[0, 0:NX - 1], xslot + (z - zz + NZ) % NZ)

    def group(i):
        return (z // 2 + jnp.where(i == 2, 3, jnp.where(i == 3, 2, i))) % 4

    def to_row(buf, slot):
        loop(1, NY, lambda d: send_to(buf.at[y, k], buf.at[y, k], y_peer(d), slot, slot))

    def to_sibling(buf, slot):
        send_to(buf.at[:, k], buf.at[:, k], sibling, slot, slot)

    def sum_core(part, cb, slot):
        send_to(part.at[:, 1 - k], cb, sibling, slot, slot)

    def sum_y(part, cb, sb, yb, slot, into):
        landed(cb, slot)
        sb[...] = part[:, k] + cb[...]
        yb[y] = sb[y]
        loop(1, NY, lambda d: send_to(sb.at[(y + d) % NY], yb.at[y], y_peer(d), into, into))

    def sum_z(yb, zb, slot):
        landed(yb.at[0:NY - 1], slot + 1)
        zb[z] = jnp.sum(yb[...], axis=0)
        loop(1, NZ, lambda d: send_to(zb.at[z], zb.at[z], z_peer(d), slot + 2, slot + 2))

    def sum_x(zb, xb, slot):
        landed(zb.at[0:NZ - 1], slot + 2)
        xb[x] = jnp.sum(zb[...], axis=0)
        loop(1, NX, lambda d: send_to(xb.at[x], xb.at[x], x_peer(d), slot + 3, slot + 3))

    def sum_back_y(xb, full, slot):
        landed(xb.at[0:NX - 1], slot + 3)
        full[y, k] = jnp.sum(xb[...], axis=0)
        to_row(full, slot + 4)

    def sum_back_core(full, slot):
        landed(full.at[0:NY - 1, 0], slot + 4)
        to_sibling(full, slot + 5)

    def sum_end(full, slot):
        landed(full.at[:, 0], slot + 5)

    def turn(g):
        at_v[g] = a_v[pl.ds(2 * g, 2)].reshape(256, 512).T

    perm(pv, pc.at[r2 // 2, r2 % 2], (r2, c2), P_PERM)
    gather_start(pr, P_Z, P_X)
    sum_core(gpart, gcb, G_SUM)
    a_copy.wait()
    turn(0)
    gather_forward(pr, P_Z, P_X, 0, 2)
    sum_y(gpart, gcb, gs, gyb, G_SUM, G_SUM + 1)
    gather_forward(pr, P_Z, P_X, 2, 4)
    landed(pc.at[0, 0], P_PERM)
    to_row(pc, P_Y)
    gather_forward(pr, P_Z, P_X, 4, 7)
    turn(1)
    sum_z(gyb, gzb, G_SUM)
    loop(2, 4, turn)
    landed(pc.at[0:NY - 1, 0], P_Y)
    to_sibling(pc, P_CORE)
    sum_x(gzb, gxb, G_SUM)

    def share(i):
        g = group(i)
        gather_wait(pr, P_X, g)

        def half(h):
            rows = pl.ds(pl.multiple_of(h * 256, 256), 256)
            part = nn(at_v[g, rows, :], pr[pl.ds(2 * g, 2)].reshape(256, B)).reshape(4, 2, H, B)
            place = pl.ds(h * 4, 4)

            @pl.when(i == 0)
            def _():
                zpart[place] = part

            @pl.when(i > 0)
            def _():
                zpart[place] = zpart[place] + part
        loop(0, 2, half)
    loop(0, 4, share)
    send_to(zpart.at[:, 1 - k], zcb, sibling, Z_CORE, Z_CORE)
    landed(pc.at[:, 0], P_CORE)
    pct[...] = pc[...].reshape(NR * H, B).T
    mpart[...] = nn(pct[...], zpart[...].reshape(NR * H, B)).reshape(NY, 2, G16, B)
    sum_core(mpart, mcb, M_SUM)
    sum_back_y(gxb, gf, G_SUM)
    sum_y(zpart, zcb, zs, zyb, Z_CORE, Z_Y)
    sum_y(mpart, mcb, ms, myb, M_SUM, M_SUM + 1)
    sum_back_core(gf, G_SUM)

    lane = lax.broadcasted_iota(jnp.int32, (128, 128), 1)
    subl = lax.broadcasted_iota(jnp.int32, (128, 128), 0)

    def sweep(lo, hi):
        def body(j, a):
            in_col = lane == j
            in_row = subl == j
            col = jnp.sum(jnp.where(in_col, a, 0.0), axis=1, keepdims=True)
            row = jnp.sum(jnp.where(in_row, a, 0.0), axis=0, keepdims=True)
            piv = jnp.sum(jnp.where(lane[0:1] == j, row, 0.0), axis=1, keepdims=True)
            inv = 1.0 / piv
            scaled = row * inv
            other = a - col * scaled
            other = jnp.where(in_col, col * inv, other)
            return jnp.where(in_row, jnp.where(in_col, -inv, scaled), other)
        blk[...] = lax.fori_loop(lo, hi, body, blk[...])

    sum_end(gf, G_SUM)
    w[...] = gf[...].reshape(B, B)
    blk[...] = w[0:128, 0:128]
    sweep(0, 32)
    landed(zyb.at[0:NY - 1], Z_Y)
    zc[y, k] = jnp.sum(zyb[...], axis=0)
    perm(zc.at[y, k], zr.at[c1 // NX, c1 % NX], (r1, c1), Z_PERM)
    to_row(zc, ZC_Y)
    sum_z(myb, mzb, M_SUM)
    sweep(32, 64)
    landed(zr.at[0, 0], Z_PERM)
    gather_start(zr, Z_Z, Z_X)
    sweep(64, 80)
    gather_forward(zr, Z_Z, Z_X, 0, 2)
    sum_x(mzb, mxb, M_SUM)
    gather_forward(zr, Z_Z, Z_X, 2, 4)
    landed(zc.at[0:NY - 1, 0], ZC_Y)
    to_sibling(zc, ZC_CORE)
    sweep(80, 96)
    sum_back_y(mxb, mf, M_SUM)
    gather_forward(zr, Z_Z, Z_X, 4, 7)
    sweep(96, 128)
    sum_back_core(mf, M_SUM)
    sub[...] = nn(w[128:256, 0:128], -blk[...])
    w[0:128, 0:128] = -blk[...]
    blk[...] = w[128:256, 128:256] - nt(sub[...], w[128:256, 0:128])
    sweep(0, 128)
    low = nn(blk[...], sub[...])
    w[128:256, 128:256] = -blk[...]
    w[128:256, 0:128] = low
    w[0:128, 128:256] = low.T
    w[0:128, 0:128] = w[0:128, 0:128] - tn(sub[...], low)
    yc[...] = nt(w[...], pc[...].reshape(NR * H, B))
    sum_end(mf, M_SUM)
    rest = nn(mf[...].reshape(B, B), yc[...])
    landed(zc.at[:, 0], ZC_CORE)
    xc[...] = nt(w[...], zc[...].reshape(NR * H, B)) - nn(w[...], rest)

    def out_copy(g):
        place = pl.ds(2 * g, 2)
        return pltpu.make_async_copy(o_v.at[place], out_hbm.at[place], local.at[g])

    def update(i):
        g = group(i)
        gather_wait(zr, Z_X, g)
        place = pl.ds(2 * g, 2)
        change = nn(pr[place].reshape(256, B), xc[...]) + nn(zr[place].reshape(256, B), yc[...])
        rows = r * 1024 + g * 256 + lax.broadcasted_iota(jnp.int32, (256, 512), 0)
        cols = c * 512 + lax.broadcasted_iota(jnp.int32, (256, 512), 1)
        old = a_v[place].reshape(256, 512)
        o_v[place] = jnp.where(rows >= cols, old - change, old).reshape(2, NX, H, 512)
        out_copy(g).start()
    loop(0, 4, update)

    for slot in (P_Z, Z_Z):
        left(pr.at[0:NZ - 1, 0], slot)
    for slot in (P_X, Z_X):
        left(pr.at[:, 0:NX - 1], slot)
    for slot in (P_Y, Z_Y, ZC_Y):
        left(pc.at[0:NY - 1, 0], slot)
    for slot in (P_CORE, Z_CORE, ZC_CORE):
        left(pc.at[:, 0], slot)
    for slot in (G_SUM, M_SUM):
        left(gf.at[:, 0], slot)
        left(gf.at[0:NY - 1, 0], slot + 1)
        left(gf.at[0:NZ - 1, 0], slot + 2)
        left(gf.at[0:NX - 1, 0], slot + 3)
        left(gf.at[0:NY - 1, 0], slot + 4)
        left(gf.at[:, 0], slot + 5)

    @pl.when(jnp.logical_not(alone))
    def _():
        left(pc.at[0, 0], P_PERM)
        left(pc.at[0, 0], Z_PERM)

    loop(0, 4, lambda g: out_copy(g).wait())


def on_device(matrix, panel):
    vm = lambda *s: pltpu.VMEM(s, F32)
    sums = [vm(NY, 2, G16, B), vm(NY, G16, B), vm(NY, G16, B), vm(NY, G16, B), vm(NZ, G16, B), vm(NX, G16, B),
            vm(NY, 2, G16, B)]
    out = pl.pallas_call(
        kernel,
        out_shape=jax.ShapeDtypeStruct((NZ, NX, H, 512), F32),
        in_specs=[pl.BlockSpec(memory_space=pltpu.HBM), pl.BlockSpec(memory_space=pltpu.HBM)],
        out_specs=pl.BlockSpec(memory_space=pltpu.HBM),
        scratch_shapes=[
            vm(NZ, NX, H, 512), vm(4, 512, 256), vm(NZ, NX, H, 512), vm(H, B),
            vm(NZ, NX, H, B), vm(NZ, NX, H, B), vm(NY, 2, H, B), vm(B, NR * H), vm(NY, 2, H, B),
            vm(NY, 2, H, B), vm(NY, H, B), vm(NY, H, B), vm(NY, H, B),
            *sums, *sums,
            vm(B, B), vm(128, 128), vm(128, 128), vm(B, 512), vm(B, 512),
            pltpu.SemaphoreType.DMA((SEMS,)), pltpu.SemaphoreType.DMA((SEMS,)), pltpu.SemaphoreType.DMA((5,)),
        ],
        compiler_params=pltpu.CompilerParams(
            collective_id=0, has_side_effects=True, vmem_limit_bytes=60 * 1024 * 1024),
        cost_estimate=pl.CostEstimate(flops=8 * 10**9, bytes_accessed=8 * 2**20, transcendentals=0),
    )(matrix.reshape(NZ, NX, H, 512), panel)
    return out.reshape(1024, 512)


def solution(mesh):
    return jax.shard_map(
        on_device,
        mesh=mesh,
        in_specs=(P("row", "col"), P(("row", "col"), None)),
        out_specs=P("row", "col"),
        check_vma=False,
    )
```

```python
import jax
import jax.numpy as jnp
from jax import lax
from jax.experimental import pallas as pl
from jax.experimental.pallas import tpu as pltpu
from jax.sharding import PartitionSpec as P

HIGH = lax.Precision.HIGHEST
MESH = pl.DeviceIdType.MESH
F32 = jnp.float32
NX, NY, NZ, NR = 4, 8, 8, 16
H = 32
B = 256
G16 = 16
P_Z, P_X, Z_Z, Z_X = 0, 8, 16, 24
P_PERM, P_Y, P_CORE, Z_CORE, Z_Y, Z_PERM, ZC_Y, ZC_CORE = 32, 33, 34, 35, 36, 37, 38, 39
G_SUM, M_SUM = 40, 46
SEMS = 52


def nn(a, b):
    return jnp.dot(a, b, precision=HIGH, preferred_element_type=F32)


def nt(a, b):
    return lax.dot_general(a, b, (((1,), (1,)), ((), ())), precision=HIGH, preferred_element_type=F32)


def tn(a, b):
    return lax.dot_general(a, b, (((0,), (0,)), ((), ())), precision=HIGH, preferred_element_type=F32)


def split(a):
    high = a.astype(jnp.bfloat16)
    return high, (a - high.astype(F32)).astype(jnp.bfloat16)


def three(a, b):
    def one(u, v):
        return jnp.dot(u, v, preferred_element_type=F32)
    return one(a[0], b[0]) + (one(a[1], b[0]) + one(a[0], b[1]))


def kernel(a_hbm, p_hbm, out_hbm, a_v, at_hi, at_lo, o_v, pv, pr, zr, pc, pct, zc, zpart, zcb, zs, zyb,
           gpart, gcb, gs, gyb, gzb, gxb, gf, mpart, mcb, ms, myb, mzb, mxb, mf, w, blk, sub, xc, xh, xl, yc, yh, yl, send, recv, local):
    r = lax.axis_index("row")
    c = lax.axis_index("col")
    y = r // 2
    k = r % 2
    z = c // NX
    x = c % NX
    r2, c2 = c % NR, 2 * r + c // NR
    r1, c1 = c // 2, (c % 2) * NR + r
    alone = jnp.logical_and(r2 == r, c2 == c)
    sibling = (2 * y + 1 - k, c)

    def z_peer(d):
        return (r, (z + d) % NZ * NX + x)

    def x_peer(d):
        return (r, z * NX + (x + d) % NX)

    def y_peer(d):
        return ((y + d) % NY * 2 + k, c)

    def send_to(src, dst, device, out_slot, in_slot):
        pltpu.make_async_remote_copy(
            src_ref=src, dst_ref=dst, send_sem=send.at[out_slot], recv_sem=recv.at[in_slot],
            device_id=device, device_id_type=MESH).start()

    def loop(lo, hi, step):
        def body(d, carry):
            step(d)
            return carry
        lax.fori_loop(lo, hi, body, 0)

    def landed(ref, slot):
        pltpu.make_async_copy(ref, ref, recv.at[slot]).wait()

    def left(ref, slot):
        pltpu.make_async_copy(ref, ref, send.at[slot]).wait()

    barrier = pltpu.get_barrier_semaphore()

    def greet(device):
        pl.semaphore_signal(barrier, inc=1, device_id=device, device_id_type=MESH)

    loop(1, NZ, lambda d: greet(z_peer(d)))
    loop(1, NX, lambda d: greet(x_peer(d)))
    loop(1, NY, lambda d: greet(y_peer(d)))
    greet(sibling)

    @pl.when(jnp.logical_not(alone))
    def _():
        greet((r2, c2))
        greet((r1, c1))

    p_copy = pltpu.make_async_copy(p_hbm, pv, local.at[4])
    a_copy = pltpu.make_async_copy(a_hbm, a_v, local.at[0])
    p_copy.start()
    a_copy.start()
    p_copy.wait()
    pr[z, x] = pv[...]
    gpart[...] = tn(pv[...], pv[...]).reshape(NY, 2, G16, B)
    pl.semaphore_wait(barrier, NZ - 1 + NX - 1 + NY - 1 + 1 + jnp.where(alone, 0, 2))

    def perm(src, dst, device, slot):
        @pl.when(alone)
        def _():
            pltpu.make_async_copy(src, dst, recv.at[slot]).start()

        @pl.when(jnp.logical_not(alone))
        def _():
            send_to(src, dst, device, slot, slot)

    def order(j):
        return jnp.where(j % 2 == 0, j // 2 + 1, NZ - 1 - j // 2)

    def gather_start(buf, zslot, xslot):
        loop(0, NZ - 1, lambda j: send_to(buf.at[z, x], buf.at[z, x], z_peer(order(j)), zslot, zslot + order(j)))
        loop(1, NX, lambda e: send_to(buf.at[z, x], buf.at[z, x], x_peer(e), xslot, xslot))

    def gather_forward(buf, zslot, xslot, lo, hi):
        def step(j):
            d = order(j)
            zz = (z - d + NZ) % NZ
            landed(buf.at[zz, x], zslot + d)
            loop(1, NX, lambda e: send_to(buf.at[zz, x], buf.at[zz, x], x_peer(e), xslot, xslot + d))
        loop(lo, hi, step)

    def gather_wait(buf, xslot, g):
        for i in range(2):
            zz = 2 * g + i
            landed(buf.at[0, 0:NX - 1], xslot + (z - zz + NZ) % NZ)

    def group(i):
        return (z // 2 + jnp.where(i == 2, 3, jnp.where(i == 3, 2, i))) % 4

    def to_row(buf, slot):
        loop(1, NY, lambda d: send_to(buf.at[y, k], buf.at[y, k], y_peer(d), slot, slot))

    def to_sibling(buf, slot):
        send_to(buf.at[:, k], buf.at[:, k], sibling, slot, slot)

    def sum_core(part, cb, slot):
        send_to(part.at[:, 1 - k], cb, sibling, slot, slot)

    def sum_y(part, cb, sb, yb, slot, into):
        landed(cb, slot)
        sb[...] = part[:, k] + cb[...]
        yb[y] = sb[y]
        loop(1, NY, lambda d: send_to(sb.at[(y + d) % NY], yb.at[y], y_peer(d), into, into))

    def sum_z(yb, zb, slot):
        landed(yb.at[0:NY - 1], slot + 1)
        zb[z] = jnp.sum(yb[...], axis=0)
        loop(1, NZ, lambda d: send_to(zb.at[z], zb.at[z], z_peer(d), slot + 2, slot + 2))

    def sum_x(zb, xb, slot):
        landed(zb.at[0:NZ - 1], slot + 2)
        xb[x] = jnp.sum(zb[...], axis=0)
        loop(1, NX, lambda d: send_to(xb.at[x], xb.at[x], x_peer(d), slot + 3, slot + 3))

    def sum_back_y(xb, full, slot):
        landed(xb.at[0:NX - 1], slot + 3)
        full[y, k] = jnp.sum(xb[...], axis=0)
        to_row(full, slot + 4)

    def sum_back_core(full, slot):
        landed(full.at[0:NY - 1, 0], slot + 4)
        to_sibling(full, slot + 5)

    def sum_end(full, slot):
        landed(full.at[:, 0], slot + 5)

    def turn(g):
        at_hi[g], at_lo[g] = split(a_v[pl.ds(2 * g, 2)].reshape(256, 512).T)

    sum_core(gpart, gcb, G_SUM)
    gather_start(pr, P_Z, P_X)
    perm(pv, pc.at[r2 // 2, r2 % 2], (r2, c2), P_PERM)
    a_copy.wait()
    turn(0)
    gather_forward(pr, P_Z, P_X, 0, 2)
    sum_y(gpart, gcb, gs, gyb, G_SUM, G_SUM + 1)
    gather_forward(pr, P_Z, P_X, 2, 4)
    landed(pc.at[0, 0], P_PERM)
    to_row(pc, P_Y)
    gather_forward(pr, P_Z, P_X, 4, 7)
    turn(1)
    sum_z(gyb, gzb, G_SUM)
    loop(2, 4, turn)
    landed(pc.at[0:NY - 1, 0], P_Y)
    to_sibling(pc, P_CORE)

    def share(i):
        g = group(i)
        gather_wait(pr, P_X, g)
        panel = split(pr[pl.ds(2 * g, 2)].reshape(256, B))

        def half(h):
            rows = pl.ds(pl.multiple_of(h * 256, 256), 256)
            part = three((at_hi[g, rows, :], at_lo[g, rows, :]), panel).reshape(4, 2, H, B)
            place = pl.ds(h * 4, 4)

            @pl.when(i == 0)
            def _():
                zpart[place] = part

            @pl.when(i > 0)
            def _():
                zpart[place] = zpart[place] + part
        loop(0, 2, half)
    loop(0, 2, share)
    sum_x(gzb, gxb, G_SUM)
    loop(2, 4, share)
    send_to(zpart.at[:, 1 - k], zcb, sibling, Z_CORE, Z_CORE)
    landed(pc.at[:, 0], P_CORE)
    pct[...] = pc[...].reshape(NR * H, B).T
    sum_back_y(gxb, gf, G_SUM)
    sum_y(zpart, zcb, zs, zyb, Z_CORE, Z_Y)
    mpart[...] = nn(pct[...], zpart[...].reshape(NR * H, B)).reshape(NY, 2, G16, B)
    sum_core(mpart, mcb, M_SUM)
    sum_back_core(gf, G_SUM)
    sum_y(mpart, mcb, ms, myb, M_SUM, M_SUM + 1)

    lane = lax.broadcasted_iota(jnp.int32, (128, 128), 1)
    subl = lax.broadcasted_iota(jnp.int32, (128, 128), 0)
    lane1 = lane[0:1]
    subl1 = subl[:, 0:1]

    def sweep(lo, hi):
        def body(i, a):
            j = 2 * i
            c_0, c_1 = lane == j, lane == j + 1
            r_0, r_1 = subl == j, subl == j + 1
            col0 = jnp.sum(jnp.where(c_0, a, 0.0), axis=1, keepdims=True)
            col1 = jnp.sum(jnp.where(c_1, a, 0.0), axis=1, keepdims=True)
            row0 = jnp.sum(jnp.where(r_0, a, 0.0), axis=0, keepdims=True)
            row1 = jnp.sum(jnp.where(r_1, a, 0.0), axis=0, keepdims=True)
            p = jnp.sum(jnp.where(lane1 == j, row0, 0.0), axis=1, keepdims=True)
            q = jnp.sum(jnp.where(lane1 == j + 1, row0, 0.0), axis=1, keepdims=True)
            s = jnp.sum(jnp.where(lane1 == j + 1, row1, 0.0), axis=1, keepdims=True)
            ip = 1.0 / p
            t = q * ip
            i11 = 1.0 / (s - q * t)
            i01 = -t * i11
            i00 = ip - t * i01
            row0 = jnp.where(lane1 == j, -1.0, jnp.where(lane1 == j + 1, 0.0, row0))
            row1 = jnp.where(lane1 == j, 0.0, jnp.where(lane1 == j + 1, -1.0, row1))
            col0 = jnp.where(subl1 == j, -1.0, jnp.where(subl1 == j + 1, 0.0, col0))
            col1 = jnp.where(subl1 == j, 0.0, jnp.where(subl1 == j + 1, -1.0, col1))
            y0 = i00 * row0 + i01 * row1
            y1 = i01 * row0 + i11 * row1
            keep = jnp.where(c_0 | c_1 | r_0 | r_1, 0.0, a)
            return keep - col0 * y0 - col1 * y1
        blk[...] = lax.fori_loop(lo, hi, body, blk[...])

    sum_end(gf, G_SUM)
    w[...] = gf[...].reshape(B, B)
    blk[...] = w[0:128, 0:128]
    sweep(0, 14)
    landed(zyb.at[0:NY - 1], Z_Y)
    zc[y, k] = jnp.sum(zyb[...], axis=0)
    perm(zc.at[y, k], zr.at[c1 // NX, c1 % NX], (r1, c1), Z_PERM)
    to_row(zc, ZC_Y)
    sweep(14, 18)
    sum_z(myb, mzb, M_SUM)
    sweep(18, 40)
    landed(zr.at[0, 0], Z_PERM)
    gather_start(zr, Z_Z, Z_X)
    sweep(40, 52)
    gather_forward(zr, Z_Z, Z_X, 0, 2)
    sum_x(mzb, mxb, M_SUM)
    gather_forward(zr, Z_Z, Z_X, 2, 4)
    landed(zc.at[0:NY - 1, 0], ZC_Y)
    to_sibling(zc, ZC_CORE)
    sweep(52, 58)
    sum_back_y(mxb, mf, M_SUM)
    gather_forward(zr, Z_Z, Z_X, 4, 7)
    sweep(58, 64)
    sub[...] = nn(w[128:256, 0:128], -blk[...])
    w[0:128, 0:128] = -blk[...]
    blk[...] = w[128:256, 128:256] - nt(sub[...], w[128:256, 0:128])
    sweep(0, 16)
    sum_back_core(mf, M_SUM)
    sweep(16, 64)
    low = nn(blk[...], sub[...])
    w[128:256, 128:256] = -blk[...]
    w[128:256, 0:128] = low
    w[0:128, 128:256] = low.T
    w[0:128, 0:128] = w[0:128, 0:128] - tn(sub[...], low)
    yc[...] = nt(w[...], pc[...].reshape(NR * H, B))
    yh[...], yl[...] = split(yc[...])
    sum_end(mf, M_SUM)
    rest = nn(mf[...].reshape(B, B), yc[...])
    landed(zc.at[:, 0], ZC_CORE)
    xc[...] = nt(w[...], zc[...].reshape(NR * H, B)) - nn(w[...], rest)
    xh[...], xl[...] = split(xc[...])

    def out_copy(g):
        place = pl.ds(2 * g, 2)
        return pltpu.make_async_copy(o_v.at[place], out_hbm.at[place], local.at[g])

    def update(i):
        g = group(i)
        gather_wait(zr, Z_X, g)
        place = pl.ds(2 * g, 2)
        change = three(split(pr[place].reshape(256, B)), (xh[...], xl[...]))
        change += three(split(zr[place].reshape(256, B)), (yh[...], yl[...]))
        rows = r * 1024 + g * 256 + lax.broadcasted_iota(jnp.int32, (256, 512), 0)
        cols = c * 512 + lax.broadcasted_iota(jnp.int32, (256, 512), 1)
        old = a_v[place].reshape(256, 512)
        o_v[place] = jnp.where(rows >= cols, old - change, old).reshape(2, NX, H, 512)
        out_copy(g).start()
    loop(0, 4, update)

    for slot in (P_Z, Z_Z):
        left(pr.at[0:NZ - 1, 0], slot)
    for slot in (P_X, Z_X):
        left(pr.at[:, 0:NX - 1], slot)
    for slot in (P_Y, Z_Y, ZC_Y):
        left(pc.at[0:NY - 1, 0], slot)
    for slot in (P_CORE, Z_CORE, ZC_CORE):
        left(pc.at[:, 0], slot)
    for slot in (G_SUM, M_SUM):
        left(gf.at[:, 0], slot)
        left(gf.at[0:NY - 1, 0], slot + 1)
        left(gf.at[0:NZ - 1, 0], slot + 2)
        left(gf.at[0:NX - 1, 0], slot + 3)
        left(gf.at[0:NY - 1, 0], slot + 4)
        left(gf.at[:, 0], slot + 5)

    @pl.when(jnp.logical_not(alone))
    def _():
        left(pc.at[0, 0], P_PERM)
        left(pc.at[0, 0], Z_PERM)

    loop(0, 4, lambda g: out_copy(g).wait())


def on_device(matrix, panel):
    vm = lambda *s: pltpu.VMEM(s, F32)
    bf = lambda *s: pltpu.VMEM(s, jnp.bfloat16)
    sums = [vm(NY, 2, G16, B), vm(NY, G16, B), vm(NY, G16, B), vm(NY, G16, B), vm(NZ, G16, B), vm(NX, G16, B),
            vm(NY, 2, G16, B)]
    out = pl.pallas_call(
        kernel,
        out_shape=jax.ShapeDtypeStruct((NZ, NX, H, 512), F32),
        in_specs=[pl.BlockSpec(memory_space=pltpu.HBM), pl.BlockSpec(memory_space=pltpu.HBM)],
        out_specs=pl.BlockSpec(memory_space=pltpu.HBM),
        scratch_shapes=[
            vm(NZ, NX, H, 512), bf(4, 512, 256), bf(4, 512, 256), vm(NZ, NX, H, 512), vm(H, B),
            vm(NZ, NX, H, B), vm(NZ, NX, H, B), vm(NY, 2, H, B), vm(B, NR * H), vm(NY, 2, H, B),
            vm(NY, 2, H, B), vm(NY, H, B), vm(NY, H, B), vm(NY, H, B),
            *sums, *sums,
            vm(B, B), vm(128, 128), vm(128, 128), vm(B, 512), bf(B, 512), bf(B, 512), vm(B, 512), bf(B, 512), bf(B, 512),
            pltpu.SemaphoreType.DMA((SEMS,)), pltpu.SemaphoreType.DMA((SEMS,)), pltpu.SemaphoreType.DMA((5,)),
        ],
        compiler_params=pltpu.CompilerParams(
            collective_id=0, has_side_effects=True, vmem_limit_bytes=50 * 1024 * 1024),
        cost_estimate=pl.CostEstimate(flops=8 * 10**9, bytes_accessed=8 * 2**20, transcendentals=0),
    )(matrix.reshape(NZ, NX, H, 512), panel)
    return out.reshape(1024, 512)


def solution(mesh):
    return jax.shard_map(
        on_device,
        mesh=mesh,
        in_specs=(P("row", "col"), P(("row", "col"), None)),
        out_specs=P("row", "col"),
        check_vma=False,
    )
```

```python
import jax
import jax.numpy as jnp
from jax import lax
from jax.experimental import pallas as pl
from jax.experimental.pallas import tpu as pltpu
from jax.sharding import PartitionSpec as P

HIGH = lax.Precision.HIGHEST
MESH = pl.DeviceIdType.MESH
F32 = jnp.float32
NX, NY, NZ, NR = 4, 8, 8, 16
H = 32
B = 256
G16 = 16
P_Z, P_X, Z_Z, Z_X = 0, 8, 16, 24
P_PERM, P_Y, P_CORE, Z_CORE, Z_Y, Z_PERM, ZC_Y, ZC_CORE = 32, 33, 34, 35, 36, 37, 38, 39
G_SUM, M_SUM = 40, 46
SEMS = 52


def nn(a, b):
    return jnp.dot(a, b, precision=HIGH, preferred_element_type=F32)


def nt(a, b):
    return lax.dot_general(a, b, (((1,), (1,)), ((), ())), precision=HIGH, preferred_element_type=F32)


def tn(a, b):
    return lax.dot_general(a, b, (((0,), (0,)), ((), ())), precision=HIGH, preferred_element_type=F32)


def split(a):
    high = a.astype(jnp.bfloat16)
    return high, (a - high.astype(F32)).astype(jnp.bfloat16)


def three(a, b):
    def one(u, v):
        return jnp.dot(u, v, preferred_element_type=F32)
    return one(a[0], b[0]) + (one(a[1], b[0]) + one(a[0], b[1]))


def kernel(a_hbm, p_hbm, out_hbm, a_v, at_hi, at_lo, o_v, pv, pr, zr, pc, pct, zc, zpart, zcb, zs, zyb,
           gpart, gcb, gs, gyb, gzb, gxb, gf, mpart, mcb, ms, myb, mzb, mxb, mf, w, blk, sub, xc, xh, xl, yc, yh, yl, send, recv, local):
    r = lax.axis_index("row")
    c = lax.axis_index("col")
    y = r // 2
    k = r % 2
    z = c // NX
    x = c % NX
    r2, c2 = c % NR, 2 * r + c // NR
    r1, c1 = c // 2, (c % 2) * NR + r
    alone = jnp.logical_and(r2 == r, c2 == c)
    sibling = (2 * y + 1 - k, c)

    def z_peer(d):
        return (r, (z + d) % NZ * NX + x)

    def x_peer(d):
        return (r, z * NX + (x + d) % NX)

    def y_peer(d):
        return ((y + d) % NY * 2 + k, c)

    def send_to(src, dst, device, out_slot, in_slot):
        pltpu.make_async_remote_copy(
            src_ref=src, dst_ref=dst, send_sem=send.at[out_slot], recv_sem=recv.at[in_slot],
            device_id=device, device_id_type=MESH).start()

    def loop(lo, hi, step):
        def body(d, carry):
            step(d)
            return carry
        lax.fori_loop(lo, hi, body, 0)

    def landed(ref, slot):
        pltpu.make_async_copy(ref, ref, recv.at[slot]).wait()

    def left(ref, slot):
        pltpu.make_async_copy(ref, ref, send.at[slot]).wait()

    barrier = pltpu.get_barrier_semaphore()

    def greet(device):
        pl.semaphore_signal(barrier, inc=1, device_id=device, device_id_type=MESH)

    loop(1, NZ, lambda d: greet(z_peer(d)))
    loop(1, NX, lambda d: greet(x_peer(d)))
    loop(1, NY, lambda d: greet(y_peer(d)))
    greet(sibling)

    @pl.when(jnp.logical_not(alone))
    def _():
        greet((r2, c2))
        greet((r1, c1))

    p_copy = pltpu.make_async_copy(p_hbm, pv, local.at[4])
    a_copy = pltpu.make_async_copy(a_hbm, a_v, local.at[0])
    p_copy.start()
    a_copy.start()
    p_copy.wait()
    pr[z, x] = pv[...]
    gpart[...] = tn(pv[...], pv[...]).reshape(NY, 2, G16, B)
    pl.semaphore_wait(barrier, NZ - 1 + NX - 1 + NY - 1 + 1 + jnp.where(alone, 0, 2))

    def perm(src, dst, device, slot):
        @pl.when(alone)
        def _():
            pltpu.make_async_copy(src, dst, recv.at[slot]).start()

        @pl.when(jnp.logical_not(alone))
        def _():
            send_to(src, dst, device, slot, slot)

    def order(j):
        return jnp.where(j % 2 == 0, j // 2 + 1, NZ - 1 - j // 2)

    def gather_start(buf, zslot, xslot):
        loop(0, NZ - 1, lambda j: send_to(buf.at[z, x], buf.at[z, x], z_peer(order(j)), zslot, zslot + order(j)))
        loop(1, NX, lambda e: send_to(buf.at[z, x], buf.at[z, x], x_peer(e), xslot, xslot))

    def gather_forward(buf, zslot, xslot, lo, hi):
        def step(j):
            d = order(j)
            zz = (z - d + NZ) % NZ
            landed(buf.at[zz, x], zslot + d)
            loop(1, NX, lambda e: send_to(buf.at[zz, x], buf.at[zz, x], x_peer(e), xslot, xslot + d))
        loop(lo, hi, step)

    def gather_wait(buf, xslot, g):
        for i in range(2):
            zz = 2 * g + i
            landed(buf.at[0, 0:NX - 1], xslot + (z - zz + NZ) % NZ)

    def group(i):
        return (z // 2 + jnp.where(i == 2, 3, jnp.where(i == 3, 2, i))) % 4

    def to_row(buf, slot):
        loop(1, NY, lambda d: send_to(buf.at[y, k], buf.at[y, k], y_peer(d), slot, slot))

    def to_sibling(buf, slot):
        send_to(buf.at[:, k], buf.at[:, k], sibling, slot, slot)

    def sum_core(part, cb, slot):
        send_to(part.at[:, 1 - k], cb, sibling, slot, slot)

    def sum_y(part, cb, sb, yb, slot, into):
        landed(cb, slot)
        sb[...] = part[:, k] + cb[...]
        yb[y] = sb[y]
        loop(1, NY, lambda d: send_to(sb.at[(y + d) % NY], yb.at[y], y_peer(d), into, into))

    def sum_z(src, count, came, zb, slot):
        landed(src.at[0:count - 1], came)
        zb[z] = jnp.sum(src[...], axis=0)
        loop(1, NZ, lambda d: send_to(zb.at[z], zb.at[z], z_peer(d), slot + 2, slot + 2))

    def sum_x(src, count, came, xb, slot):
        landed(src.at[0:count - 1], came)
        xb[x] = jnp.sum(src[...], axis=0)
        loop(1, NX, lambda d: send_to(xb.at[x], xb.at[x], x_peer(d), slot + 3, slot + 3))

    def sum_back_y(src, count, came, full, slot):
        landed(src.at[0:count - 1], came)
        full[y, k] = jnp.sum(src[...], axis=0)
        to_row(full, slot + 4)

    def sum_back_core(full, slot):
        landed(full.at[0:NY - 1, 0], slot + 4)
        to_sibling(full, slot + 5)

    def sum_end(full, slot):
        landed(full.at[:, 0], slot + 5)

    def turn(g):
        at_hi[g], at_lo[g] = split(a_v[pl.ds(2 * g, 2)].reshape(256, 512).T)

    sum_core(gpart, gcb, G_SUM)
    gather_start(pr, P_Z, P_X)
    perm(pv, pc.at[r2 // 2, r2 % 2], (r2, c2), P_PERM)
    a_copy.wait()
    turn(0)
    gather_forward(pr, P_Z, P_X, 0, 2)
    sum_y(gpart, gcb, gs, gyb, G_SUM, G_SUM + 1)
    gather_forward(pr, P_Z, P_X, 2, 4)
    landed(pc.at[0, 0], P_PERM)
    to_row(pc, P_Y)
    gather_forward(pr, P_Z, P_X, 4, 7)
    turn(1)
    sum_z(gyb, NY, G_SUM + 1, gzb, G_SUM)
    loop(2, 4, turn)
    landed(pc.at[0:NY - 1, 0], P_Y)
    to_sibling(pc, P_CORE)

    def share(i):
        g = group(i)
        gather_wait(pr, P_X, g)
        panel = split(pr[pl.ds(2 * g, 2)].reshape(256, B))

        def half(h):
            rows = pl.ds(pl.multiple_of(h * 256, 256), 256)
            part = three((at_hi[g, rows, :], at_lo[g, rows, :]), panel).reshape(4, 2, H, B)
            place = pl.ds(h * 4, 4)

            @pl.when(i == 0)
            def _():
                zpart[place] = part

            @pl.when(i > 0)
            def _():
                zpart[place] = zpart[place] + part
        loop(0, 2, half)
    loop(0, 2, share)
    sum_x(gzb, NZ, G_SUM + 2, gxb, G_SUM)
    loop(2, 4, share)
    send_to(zpart.at[:, 1 - k], zcb, sibling, Z_CORE, Z_CORE)
    landed(pc.at[:, 0], P_CORE)
    pct[...] = pc[...].reshape(NR * H, B).T
    sum_back_y(gxb, NX, G_SUM + 3, gf, G_SUM)
    sum_y(zpart, zcb, zs, zyb, Z_CORE, Z_Y)
    mpart[...] = nn(pct[...], zpart[...].reshape(NR * H, B)).reshape(NY, 2, G16, B)
    sum_core(mpart, mcb, M_SUM)
    sum_back_core(gf, G_SUM)
    sum_y(mpart, mcb, ms, myb, M_SUM, M_SUM + 1)

    lane = lax.broadcasted_iota(jnp.int32, (128, 128), 1)
    subl = lax.broadcasted_iota(jnp.int32, (128, 128), 0)
    lane1 = lane[0:1]
    subl1 = subl[:, 0:1]

    def pair(p, q, s):
        ip = 1.0 / p
        t = q * ip
        i11 = 1.0 / (s - q * t)
        i01 = -t * i11
        return ip - t * i01, i01, i11

    def sweep(lo, hi):
        def step(i):
            j = 4 * i
            a = blk[...]
            rows = [blk[pl.ds(j + u, 1), :] for u in range(4)]
            cols = [jnp.sum(jnp.where(lane == j + u, a, 0.0), axis=1, keepdims=True) for u in range(4)]

            def at(u, v):
                return jnp.sum(jnp.where(lane1 == j + v, rows[u], 0.0), axis=1, keepdims=True)
            e00, e01, e11 = pair(at(0, 0), at(0, 1), at(1, 1))
            f00, f01, f10, f11 = at(0, 2), at(0, 3), at(1, 2), at(1, 3)
            t00, t01 = e00 * f00 + e01 * f10, e00 * f01 + e01 * f11
            t10, t11 = e01 * f00 + e11 * f10, e01 * f01 + e11 * f11
            g00, g01, g11 = pair(at(2, 2) - f00 * t00 - f10 * t10, at(2, 3) - f00 * t01 - f10 * t11,
                                 at(3, 3) - f01 * t01 - f11 * t11)
            b00, b01 = -(t00 * g00 + t01 * g01), -(t00 * g01 + t01 * g11)
            b10, b11 = -(t10 * g00 + t11 * g01), -(t10 * g01 + t11 * g11)
            a00, a01 = e00 - b00 * t00 - b01 * t01, e01 - b00 * t10 - b01 * t11
            a11 = e11 - b10 * t10 - b11 * t11
            inverse = ((a00, a01, b00, b01), (a01, a11, b10, b11), (b00, b10, g00, g01), (b01, b11, g01, g11))
            in_lane = (lane >= j) & (lane < j + 4)
            in_subl = (subl >= j) & (subl < j + 4)
            rows = [jnp.where(lane1 == j + u, -1.0, jnp.where(in_lane[0:1], 0.0, rows[u])) for u in range(4)]
            cols = [jnp.where(subl1 == j + u, -1.0, jnp.where((subl1 >= j) & (subl1 < j + 4), 0.0, cols[u]))
                    for u in range(4)]
            new = jnp.where(in_lane | in_subl, 0.0, a)
            for u in range(4):
                m = inverse[u]
                new -= cols[u] * (m[0] * rows[0] + m[1] * rows[1] + m[2] * rows[2] + m[3] * rows[3])
            blk[...] = new
        loop(lo, hi, step)

    sum_end(gf, G_SUM)
    w[...] = gf[...].reshape(B, B)
    blk[...] = w[0:128, 0:128]
    sweep(0, 10)
    landed(zyb.at[0:NY - 1], Z_Y)
    zc[y, k] = jnp.sum(zyb[...], axis=0)
    perm(zc.at[y, k], zr.at[c1 // NX, c1 % NX], (r1, c1), Z_PERM)
    to_row(zc, ZC_Y)
    sweep(10, 13)
    sum_x(myb, NY, M_SUM + 1, mxb, M_SUM)
    sweep(13, 24)
    sum_z(mxb, NX, M_SUM + 3, mzb, M_SUM)
    sweep(24, 32)
    landed(zr.at[0, 0], Z_PERM)
    gather_start(zr, Z_Z, Z_X)
    sub[...] = nn(w[128:256, 0:128], -blk[...])
    w[0:128, 0:128] = -blk[...]
    blk[...] = w[128:256, 128:256] - nt(sub[...], w[128:256, 0:128])
    sweep(0, 7)
    gather_forward(zr, Z_Z, Z_X, 0, 4)
    landed(zc.at[0:NY - 1, 0], ZC_Y)
    to_sibling(zc, ZC_CORE)
    gather_forward(zr, Z_Z, Z_X, 4, 7)
    sum_back_y(mzb, NZ, M_SUM + 2, mf, M_SUM)
    sweep(7, 24)
    sum_back_core(mf, M_SUM)
    sweep(24, 32)
    low = nn(blk[...], sub[...])
    w[128:256, 128:256] = -blk[...]
    w[128:256, 0:128] = low
    w[0:128, 128:256] = low.T
    w[0:128, 0:128] = w[0:128, 0:128] - tn(sub[...], low)
    yc[...] = nt(w[...], pc[...].reshape(NR * H, B))
    yh[...], yl[...] = split(yc[...])
    sum_end(mf, M_SUM)
    rest = nn(mf[...].reshape(B, B), yc[...])
    landed(zc.at[:, 0], ZC_CORE)
    xc[...] = nt(w[...], zc[...].reshape(NR * H, B)) - nn(w[...], rest)
    xh[...], xl[...] = split(xc[...])

    def out_copy(g):
        place = pl.ds(2 * g, 2)
        return pltpu.make_async_copy(o_v.at[place], out_hbm.at[place], local.at[g])

    def update(i):
        g = group(i)
        gather_wait(zr, Z_X, g)
        place = pl.ds(2 * g, 2)
        change = three(split(pr[place].reshape(256, B)), (xh[...], xl[...]))
        change += three(split(zr[place].reshape(256, B)), (yh[...], yl[...]))
        rows = r * 1024 + g * 256 + lax.broadcasted_iota(jnp.int32, (256, 512), 0)
        cols = c * 512 + lax.broadcasted_iota(jnp.int32, (256, 512), 1)
        old = a_v[place].reshape(256, 512)
        o_v[place] = jnp.where(rows >= cols, old - change, old).reshape(2, NX, H, 512)
        out_copy(g).start()
    loop(0, 4, update)

    for slot in (P_Z, Z_Z):
        left(pr.at[0:NZ - 1, 0], slot)
    for slot in (P_X, Z_X):
        left(pr.at[:, 0:NX - 1], slot)
    for slot in (P_Y, Z_Y, ZC_Y):
        left(pc.at[0:NY - 1, 0], slot)
    for slot in (P_CORE, Z_CORE, ZC_CORE):
        left(pc.at[:, 0], slot)
    for slot in (G_SUM, M_SUM):
        left(gf.at[:, 0], slot)
        left(gf.at[0:NY - 1, 0], slot + 1)
        left(gf.at[0:NZ - 1, 0], slot + 2)
        left(gf.at[0:NX - 1, 0], slot + 3)
        left(gf.at[0:NY - 1, 0], slot + 4)
        left(gf.at[:, 0], slot + 5)

    @pl.when(jnp.logical_not(alone))
    def _():
        left(pc.at[0, 0], P_PERM)
        left(pc.at[0, 0], Z_PERM)

    loop(0, 4, lambda g: out_copy(g).wait())


def on_device(matrix, panel):
    vm = lambda *s: pltpu.VMEM(s, F32)
    bf = lambda *s: pltpu.VMEM(s, jnp.bfloat16)
    sums = [vm(NY, 2, G16, B), vm(NY, G16, B), vm(NY, G16, B), vm(NY, G16, B), vm(NZ, G16, B), vm(NX, G16, B),
            vm(NY, 2, G16, B)]
    out = pl.pallas_call(
        kernel,
        out_shape=jax.ShapeDtypeStruct((NZ, NX, H, 512), F32),
        in_specs=[pl.BlockSpec(memory_space=pltpu.HBM), pl.BlockSpec(memory_space=pltpu.HBM)],
        out_specs=pl.BlockSpec(memory_space=pltpu.HBM),
        scratch_shapes=[
            vm(NZ, NX, H, 512), bf(4, 512, 256), bf(4, 512, 256), vm(NZ, NX, H, 512), vm(H, B),
            vm(NZ, NX, H, B), vm(NZ, NX, H, B), vm(NY, 2, H, B), vm(B, NR * H), vm(NY, 2, H, B),
            vm(NY, 2, H, B), vm(NY, H, B), vm(NY, H, B), vm(NY, H, B),
            *sums, *sums,
            vm(B, B), vm(128, 128), vm(128, 128), vm(B, 512), bf(B, 512), bf(B, 512), vm(B, 512), bf(B, 512), bf(B, 512),
            pltpu.SemaphoreType.DMA((SEMS,)), pltpu.SemaphoreType.DMA((SEMS,)), pltpu.SemaphoreType.DMA((5,)),
        ],
        compiler_params=pltpu.CompilerParams(
            collective_id=0, has_side_effects=True, vmem_limit_bytes=50 * 1024 * 1024),
        cost_estimate=pl.CostEstimate(flops=8 * 10**9, bytes_accessed=8 * 2**20, transcendentals=0),
    )(matrix.reshape(NZ, NX, H, 512), panel)
    return out.reshape(1024, 512)


def solution(mesh):
    return jax.shard_map(
        on_device,
        mesh=mesh,
        in_specs=(P("row", "col"), P(("row", "col"), None)),
        out_specs=P("row", "col"),
        check_vma=False,
    )
```

```python
import jax
import jax.numpy as jnp
from jax import lax
from jax.experimental import pallas as pl
from jax.experimental.pallas import tpu as pltpu
from jax.sharding import PartitionSpec as P

HIGH = lax.Precision.HIGHEST
MESH = pl.DeviceIdType.MESH
F32 = jnp.float32
NX, NY, NZ, NR = 4, 8, 8, 16
H = 32
B = 256
G16 = 16
P_Z, P_X, Z_Z, Z_X = 0, 8, 16, 24
P_PERM, P_Y, P_CORE, Z_CORE, Z_Y, Z_PERM, ZC_Y, ZC_CORE = 32, 33, 34, 35, 36, 37, 38, 39
G_SUM, M_SUM = 40, 46
SEMS = 52


def nn(a, b):
    return jnp.dot(a, b, precision=HIGH, preferred_element_type=F32)


def nt(a, b):
    return lax.dot_general(a, b, (((1,), (1,)), ((), ())), precision=HIGH, preferred_element_type=F32)


def tn(a, b):
    return lax.dot_general(a, b, (((0,), (0,)), ((), ())), precision=HIGH, preferred_element_type=F32)


def split(a):
    high = a.astype(jnp.bfloat16)
    return high, (a - high.astype(F32)).astype(jnp.bfloat16)


def three(a, b):
    def one(u, v):
        return jnp.dot(u, v, preferred_element_type=F32)
    return one(a[0], b[0]) + (one(a[1], b[0]) + one(a[0], b[1]))


def kernel(a_hbm, p_hbm, out_hbm, a_v, at_hi, at_lo, o_v, pv, pr, zr, pc, pct, zc, zpart, zcb, zs, zyb,
           gpart, gcb, gs, gyb, gzb, gxb, gf, mpart, mcb, ms, myb, mzb, mxb, mf, w, blk, sub, xc, xh, xl, yc, yh, yl, send, recv, local):
    r = lax.axis_index("row")
    c = lax.axis_index("col")
    y = r // 2
    k = r % 2
    z = c // NX
    x = c % NX
    r2, c2 = c % NR, 2 * r + c // NR
    r1, c1 = c // 2, (c % 2) * NR + r
    alone = jnp.logical_and(r2 == r, c2 == c)
    sibling = (2 * y + 1 - k, c)

    def z_peer(d):
        return (r, (z + d) % NZ * NX + x)

    def x_peer(d):
        return (r, z * NX + (x + d) % NX)

    def y_peer(d):
        return ((y + d) % NY * 2 + k, c)

    def send_to(src, dst, device, out_slot, in_slot):
        pltpu.make_async_remote_copy(
            src_ref=src, dst_ref=dst, send_sem=send.at[out_slot], recv_sem=recv.at[in_slot],
            device_id=device, device_id_type=MESH).start()

    def loop(lo, hi, step):
        def body(d, carry):
            step(d)
            return carry
        lax.fori_loop(lo, hi, body, 0)

    def landed(ref, slot):
        pltpu.make_async_copy(ref, ref, recv.at[slot]).wait()

    def left(ref, slot):
        pltpu.make_async_copy(ref, ref, send.at[slot]).wait()

    barrier = pltpu.get_barrier_semaphore()

    def greet(device):
        pl.semaphore_signal(barrier, inc=1, device_id=device, device_id_type=MESH)

    loop(1, NZ, lambda d: greet(z_peer(d)))
    loop(1, NX, lambda d: greet(x_peer(d)))
    loop(1, NY, lambda d: greet(y_peer(d)))
    greet(sibling)

    @pl.when(jnp.logical_not(alone))
    def _():
        greet((r2, c2))
        greet((r1, c1))

    p_copy = pltpu.make_async_copy(p_hbm, pv, local.at[4])
    a_copy = pltpu.make_async_copy(a_hbm, a_v, local.at[0])
    p_copy.start()
    a_copy.start()
    p_copy.wait()
    pr[z, x] = pv[...]
    gpart[...] = tn(pv[...], pv[...]).reshape(NY, 2, G16, B)
    pl.semaphore_wait(barrier, NZ - 1 + NX - 1 + NY - 1 + 1 + jnp.where(alone, 0, 2))

    def perm(src, dst, device, slot):
        @pl.when(alone)
        def _():
            pltpu.make_async_copy(src, dst, recv.at[slot]).start()

        @pl.when(jnp.logical_not(alone))
        def _():
            send_to(src, dst, device, slot, slot)

    def order(j):
        return jnp.where(j % 2 == 0, j // 2 + 1, NZ - 1 - j // 2)

    def gather_start(buf, zslot, xslot):
        loop(0, NZ - 1, lambda j: send_to(buf.at[z, x], buf.at[z, x], z_peer(order(j)), zslot, zslot + order(j)))
        loop(1, NX, lambda e: send_to(buf.at[z, x], buf.at[z, x], x_peer(e), xslot, xslot))

    def gather_forward(buf, zslot, xslot, lo, hi):
        def step(j):
            d = order(j)
            zz = (z - d + NZ) % NZ
            landed(buf.at[zz, x], zslot + d)
            loop(1, NX, lambda e: send_to(buf.at[zz, x], buf.at[zz, x], x_peer(e), xslot, xslot + d))
        loop(lo, hi, step)

    def gather_wait(buf, xslot, g):
        for i in range(2):
            zz = 2 * g + i
            landed(buf.at[0, 0:NX - 1], xslot + (z - zz + NZ) % NZ)

    def group(i):
        return (z // 2 + jnp.where(i == 2, 3, jnp.where(i == 3, 2, i))) % 4

    def to_row(buf, slot):
        loop(1, NY, lambda d: send_to(buf.at[y, k], buf.at[y, k], y_peer(d), slot, slot))

    def to_sibling(buf, slot):
        send_to(buf.at[:, k], buf.at[:, k], sibling, slot, slot)

    def sum_core(part, cb, slot):
        send_to(part.at[:, 1 - k], cb, sibling, slot, slot)

    def sum_y(part, cb, sb, yb, slot, into):
        landed(cb, slot)
        sb[...] = part[:, k] + cb[...]
        yb[y] = sb[y]
        loop(1, NY, lambda d: send_to(sb.at[(y + d) % NY], yb.at[y], y_peer(d), into, into))

    def sum_z(src, count, came, zb, slot):
        landed(src.at[0:count - 1], came)
        zb[z] = jnp.sum(src[...], axis=0)
        loop(1, NZ, lambda d: send_to(zb.at[z], zb.at[z], z_peer(d), slot + 2, slot + 2))

    def sum_x(src, count, came, xb, slot):
        landed(src.at[0:count - 1], came)
        xb[x] = jnp.sum(src[...], axis=0)
        loop(1, NX, lambda d: send_to(xb.at[x], xb.at[x], x_peer(d), slot + 3, slot + 3))

    def sum_back_y(src, count, came, full, slot):
        landed(src.at[0:count - 1], came)
        full[y, k] = jnp.sum(src[...], axis=0)
        to_row(full, slot + 4)

    def scatter_z(part, cb, sb, zb, slot):
        landed(cb, slot)
        sb[...] = part[:, k] + cb[...]
        zb[z] = sb[z]
        loop(1, NZ, lambda d: send_to(sb.at[(z + d) % NZ], zb.at[z], z_peer(d), slot + 1, slot + 1))

    def middle_y(src, count, came, yb, slot):
        landed(src.at[0:count - 1], came)
        yb[y] = jnp.sum(src[...], axis=0)
        loop(1, NY, lambda d: send_to(yb.at[y], yb.at[y], y_peer(d), slot + 2, slot + 2))

    def back_z(src, count, came, full, slot):
        landed(src.at[0:count - 1], came)
        full[z, k] = jnp.sum(src[...], axis=0)
        loop(1, NZ, lambda d: send_to(full.at[z, k], full.at[z, k], z_peer(d), slot + 4, slot + 4))

    def sum_back_core(full, slot):
        landed(full.at[0:NY - 1, 0], slot + 4)
        to_sibling(full, slot + 5)

    def sum_end(full, slot):
        landed(full.at[:, 0], slot + 5)

    def turn(g):
        at_hi[g], at_lo[g] = split(a_v[pl.ds(2 * g, 2)].reshape(256, 512).T)

    sum_core(gpart, gcb, G_SUM)
    gather_start(pr, P_Z, P_X)
    perm(pv, pc.at[r2 // 2, r2 % 2], (r2, c2), P_PERM)
    a_copy.wait()
    turn(0)
    gather_forward(pr, P_Z, P_X, 0, 2)
    sum_y(gpart, gcb, gs, gyb, G_SUM, G_SUM + 1)
    gather_forward(pr, P_Z, P_X, 2, 4)
    landed(pc.at[0, 0], P_PERM)
    to_row(pc, P_Y)
    gather_forward(pr, P_Z, P_X, 4, 7)
    turn(1)
    sum_z(gyb, NY, G_SUM + 1, gzb, G_SUM)
    loop(2, 4, turn)
    landed(pc.at[0:NY - 1, 0], P_Y)
    to_sibling(pc, P_CORE)

    def share(i):
        g = group(i)
        gather_wait(pr, P_X, g)
        panel = split(pr[pl.ds(2 * g, 2)].reshape(256, B))

        def half(h):
            rows = pl.ds(pl.multiple_of(h * 256, 256), 256)
            part = three((at_hi[g, rows, :], at_lo[g, rows, :]), panel).reshape(4, 2, H, B)
            place = pl.ds(h * 4, 4)

            @pl.when(i == 0)
            def _():
                zpart[place] = part

            @pl.when(i > 0)
            def _():
                zpart[place] = zpart[place] + part
        loop(0, 2, half)
    sum_x(gzb, NZ, G_SUM + 2, gxb, G_SUM)
    loop(0, 4, share)
    send_to(zpart.at[:, 1 - k], zcb, sibling, Z_CORE, Z_CORE)
    sum_back_y(gxb, NX, G_SUM + 3, gf, G_SUM)
    landed(pc.at[:, 0], P_CORE)
    pct[...] = pc[...].reshape(NR * H, B).T
    sum_y(zpart, zcb, zs, zyb, Z_CORE, Z_Y)
    mpart[...] = nn(pct[...], zpart[...].reshape(NR * H, B)).reshape(NY, 2, G16, B)
    sum_core(mpart, mcb, M_SUM)
    sum_back_core(gf, G_SUM)
    scatter_z(mpart, mcb, ms, mzb, M_SUM)

    lane = lax.broadcasted_iota(jnp.int32, (128, 128), 1)
    subl = lax.broadcasted_iota(jnp.int32, (128, 128), 0)
    lane1 = lane[0:1]
    subl1 = subl[:, 0:1]

    def pair(p, q, s):
        ip = 1.0 / p
        t = q * ip
        i11 = 1.0 / (s - q * t)
        i01 = -t * i11
        return ip - t * i01, i01, i11

    def sweep(lo, hi):
        def step(i):
            j = 4 * i
            a = blk[...]
            rows = [blk[pl.ds(j + u, 1), :] for u in range(4)]
            cols = [jnp.sum(jnp.where(lane == j + u, a, 0.0), axis=1, keepdims=True) for u in range(4)]

            def at(u, v):
                return jnp.sum(jnp.where(lane1 == j + v, rows[u], 0.0), axis=1, keepdims=True)
            e00, e01, e11 = pair(at(0, 0), at(0, 1), at(1, 1))
            f00, f01, f10, f11 = at(0, 2), at(0, 3), at(1, 2), at(1, 3)
            t00, t01 = e00 * f00 + e01 * f10, e00 * f01 + e01 * f11
            t10, t11 = e01 * f00 + e11 * f10, e01 * f01 + e11 * f11
            g00, g01, g11 = pair(at(2, 2) - f00 * t00 - f10 * t10, at(2, 3) - f00 * t01 - f10 * t11,
                                 at(3, 3) - f01 * t01 - f11 * t11)
            b00, b01 = -(t00 * g00 + t01 * g01), -(t00 * g01 + t01 * g11)
            b10, b11 = -(t10 * g00 + t11 * g01), -(t10 * g01 + t11 * g11)
            a00, a01 = e00 - b00 * t00 - b01 * t01, e01 - b00 * t10 - b01 * t11
            a11 = e11 - b10 * t10 - b11 * t11
            inverse = ((a00, a01, b00, b01), (a01, a11, b10, b11), (b00, b10, g00, g01), (b01, b11, g01, g11))
            in_lane = (lane >= j) & (lane < j + 4)
            in_subl = (subl >= j) & (subl < j + 4)
            rows = [jnp.where(lane1 == j + u, -1.0, jnp.where(in_lane[0:1], 0.0, rows[u])) for u in range(4)]
            cols = [jnp.where(subl1 == j + u, -1.0, jnp.where((subl1 >= j) & (subl1 < j + 4), 0.0, cols[u]))
                    for u in range(4)]
            new = jnp.where(in_lane | in_subl, 0.0, a)
            for u in range(4):
                m = inverse[u]
                new -= cols[u] * (m[0] * rows[0] + m[1] * rows[1] + m[2] * rows[2] + m[3] * rows[3])
            blk[...] = new
        loop(lo, hi, step)

    sum_end(gf, G_SUM)
    w[...] = gf[...].reshape(B, B)
    blk[...] = w[0:128, 0:128]
    sweep(0, 10)
    landed(zyb.at[0:NY - 1], Z_Y)
    zc[y, k] = jnp.sum(zyb[...], axis=0)
    perm(zc.at[y, k], zr.at[c1 // NX, c1 % NX], (r1, c1), Z_PERM)
    sum_x(mzb, NZ, M_SUM + 1, mxb, M_SUM)
    sweep(10, 20)
    middle_y(mxb, NX, M_SUM + 3, myb, M_SUM)
    to_row(zc, ZC_Y)
    sweep(20, 32)
    landed(zr.at[0, 0], Z_PERM)
    gather_start(zr, Z_Z, Z_X)
    sub[...] = nn(w[128:256, 0:128], -blk[...])
    w[0:128, 0:128] = -blk[...]
    blk[...] = w[128:256, 128:256] - nt(sub[...], w[128:256, 0:128])
    sweep(0, 7)
    gather_forward(zr, Z_Z, Z_X, 0, 2)
    back_z(myb, NY, M_SUM + 2, mf, M_SUM)
    gather_forward(zr, Z_Z, Z_X, 2, 4)
    landed(zc.at[0:NY - 1, 0], ZC_Y)
    to_sibling(zc, ZC_CORE)
    gather_forward(zr, Z_Z, Z_X, 4, 7)
    sweep(7, 24)
    sum_back_core(mf, M_SUM)
    sweep(24, 32)
    low = nn(blk[...], sub[...])
    w[128:256, 128:256] = -blk[...]
    w[128:256, 0:128] = low
    w[0:128, 128:256] = low.T
    w[0:128, 0:128] = w[0:128, 0:128] - tn(sub[...], low)
    yc[...] = nt(w[...], pc[...].reshape(NR * H, B))
    yh[...], yl[...] = split(yc[...])
    sum_end(mf, M_SUM)
    rest = nn(mf[...].reshape(B, B), yc[...])
    landed(zc.at[:, 0], ZC_CORE)
    xc[...] = nt(w[...], zc[...].reshape(NR * H, B)) - nn(w[...], rest)
    xh[...], xl[...] = split(xc[...])

    def out_copy(g):
        place = pl.ds(2 * g, 2)
        return pltpu.make_async_copy(o_v.at[place], out_hbm.at[place], local.at[g])

    def update(i):
        g = group(i)
        gather_wait(zr, Z_X, g)
        place = pl.ds(2 * g, 2)
        change = three(split(pr[place].reshape(256, B)), (xh[...], xl[...]))
        change += three(split(zr[place].reshape(256, B)), (yh[...], yl[...]))
        rows = r * 1024 + g * 256 + lax.broadcasted_iota(jnp.int32, (256, 512), 0)
        cols = c * 512 + lax.broadcasted_iota(jnp.int32, (256, 512), 1)
        old = a_v[place].reshape(256, 512)
        o_v[place] = jnp.where(rows >= cols, old - change, old).reshape(2, NX, H, 512)
        out_copy(g).start()
    loop(0, 4, update)

    for slot in (P_Z, Z_Z):
        left(pr.at[0:NZ - 1, 0], slot)
    for slot in (P_X, Z_X):
        left(pr.at[:, 0:NX - 1], slot)
    for slot in (P_Y, Z_Y, ZC_Y):
        left(pc.at[0:NY - 1, 0], slot)
    for slot in (P_CORE, Z_CORE, ZC_CORE):
        left(pc.at[:, 0], slot)
    for slot in (G_SUM, M_SUM):
        left(gf.at[:, 0], slot)
        left(gf.at[0:NY - 1, 0], slot + 1)
        left(gf.at[0:NZ - 1, 0], slot + 2)
        left(gf.at[0:NX - 1, 0], slot + 3)
        left(gf.at[0:NY - 1, 0], slot + 4)
        left(gf.at[:, 0], slot + 5)

    @pl.when(jnp.logical_not(alone))
    def _():
        left(pc.at[0, 0], P_PERM)
        left(pc.at[0, 0], Z_PERM)

    loop(0, 4, lambda g: out_copy(g).wait())


def on_device(matrix, panel):
    vm = lambda *s: pltpu.VMEM(s, F32)
    bf = lambda *s: pltpu.VMEM(s, jnp.bfloat16)
    sums = [vm(NY, 2, G16, B), vm(NY, G16, B), vm(NY, G16, B), vm(NY, G16, B), vm(NZ, G16, B), vm(NX, G16, B),
            vm(NY, 2, G16, B)]
    out = pl.pallas_call(
        kernel,
        out_shape=jax.ShapeDtypeStruct((NZ, NX, H, 512), F32),
        in_specs=[pl.BlockSpec(memory_space=pltpu.HBM), pl.BlockSpec(memory_space=pltpu.HBM)],
        out_specs=pl.BlockSpec(memory_space=pltpu.HBM),
        scratch_shapes=[
            vm(NZ, NX, H, 512), bf(4, 512, 256), bf(4, 512, 256), vm(NZ, NX, H, 512), vm(H, B),
            vm(NZ, NX, H, B), vm(NZ, NX, H, B), vm(NY, 2, H, B), vm(B, NR * H), vm(NY, 2, H, B),
            vm(NY, 2, H, B), vm(NY, H, B), vm(NY, H, B), vm(NY, H, B),
            *sums, *sums,
            vm(B, B), vm(128, 128), vm(128, 128), vm(B, 512), bf(B, 512), bf(B, 512), vm(B, 512), bf(B, 512), bf(B, 512),
            pltpu.SemaphoreType.DMA((SEMS,)), pltpu.SemaphoreType.DMA((SEMS,)), pltpu.SemaphoreType.DMA((5,)),
        ],
        compiler_params=pltpu.CompilerParams(
            collective_id=0, has_side_effects=True, vmem_limit_bytes=50 * 1024 * 1024),
        cost_estimate=pl.CostEstimate(flops=8 * 10**9, bytes_accessed=8 * 2**20, transcendentals=0),
    )(matrix.reshape(NZ, NX, H, 512), panel)
    return out.reshape(1024, 512)


def solution(mesh):
    return jax.shard_map(
        on_device,
        mesh=mesh,
        in_specs=(P("row", "col"), P(("row", "col"), None)),
        out_specs=P("row", "col"),
        check_vma=False,
    )
```

```python
import jax
import jax.numpy as jnp
from jax import lax
from jax.experimental import pallas as pl
from jax.experimental.pallas import tpu as pltpu
from jax.sharding import PartitionSpec as P

HIGH = lax.Precision.HIGHEST
MESH = pl.DeviceIdType.MESH
F32 = jnp.float32
NX, NY, NZ, NR = 4, 8, 8, 16
H = 32
B = 256
G16 = 16
P_Z, P_X, Z_Z, Z_X = 0, 8, 16, 24
P_PERM, P_Y, P_CORE, Z_CORE, Z_Y, Z_PERM, ZC_Y, ZC_CORE = 32, 33, 34, 35, 36, 37, 38, 39
G_SUM, M_SUM = 40, 46
SEMS = 52


def nn(a, b):
    return jnp.dot(a, b, precision=HIGH, preferred_element_type=F32)


def nt(a, b):
    return lax.dot_general(a, b, (((1,), (1,)), ((), ())), precision=HIGH, preferred_element_type=F32)


def tn(a, b):
    return lax.dot_general(a, b, (((0,), (0,)), ((), ())), precision=HIGH, preferred_element_type=F32)


def split(a):
    high = a.astype(jnp.bfloat16)
    return high, (a - high.astype(F32)).astype(jnp.bfloat16)


def three(a, b):
    def one(u, v):
        return jnp.dot(u, v, preferred_element_type=F32)
    return one(a[0], b[0]) + (one(a[1], b[0]) + one(a[0], b[1]))


def kernel(a_hbm, p_hbm, out_hbm, a_v, at_hi, at_lo, o_v, pv, pr, zr, pc, pct, zc, zpart, zcb, zs, zyb,
           gpart, gcb, gs, gyb, gzb, gxb, gf, mpart, mcb, ms, myb, mzb, mxb, mf, w, blk, sub, xc, xh, xl, yc, yh, yl, send, recv, local):
    r = lax.axis_index("row")
    c = lax.axis_index("col")
    y = r // 2
    k = r % 2
    z = c // NX
    x = c % NX
    r2, c2 = c % NR, 2 * r + c // NR
    r1, c1 = c // 2, (c % 2) * NR + r
    alone = jnp.logical_and(r2 == r, c2 == c)
    sibling = (2 * y + 1 - k, c)

    def z_peer(d):
        return (r, (z + d) % NZ * NX + x)

    def x_peer(d):
        return (r, z * NX + (x + d) % NX)

    def y_peer(d):
        return ((y + d) % NY * 2 + k, c)

    def send_to(src, dst, device, out_slot, in_slot):
        pltpu.make_async_remote_copy(
            src_ref=src, dst_ref=dst, send_sem=send.at[out_slot], recv_sem=recv.at[in_slot],
            device_id=device, device_id_type=MESH).start()

    def loop(lo, hi, step):
        def body(d, carry):
            step(d)
            return carry
        lax.fori_loop(lo, hi, body, 0)

    def landed(ref, slot):
        pltpu.make_async_copy(ref, ref, recv.at[slot]).wait()

    def left(ref, slot):
        pltpu.make_async_copy(ref, ref, send.at[slot]).wait()

    barrier = pltpu.get_barrier_semaphore()

    def greet(device):
        pl.semaphore_signal(barrier, inc=1, device_id=device, device_id_type=MESH)

    loop(1, NZ, lambda d: greet(z_peer(d)))
    loop(1, NX, lambda d: greet(x_peer(d)))
    loop(1, NY, lambda d: greet(y_peer(d)))
    greet(sibling)

    @pl.when(jnp.logical_not(alone))
    def _():
        greet((r2, c2))
        greet((r1, c1))

    p_copy = pltpu.make_async_copy(p_hbm, pv, local.at[4])
    a_copy = pltpu.make_async_copy(a_hbm, a_v, local.at[0])
    p_copy.start()
    a_copy.start()
    p_copy.wait()
    pr[z, x] = pv[...]
    gpart[...] = tn(pv[...], pv[...]).reshape(NY, 2, G16, B)
    pl.semaphore_wait(barrier, NZ - 1 + NX - 1 + NY - 1 + 1 + jnp.where(alone, 0, 2))

    def perm(src, dst, device, slot):
        @pl.when(alone)
        def _():
            pltpu.make_async_copy(src, dst, recv.at[slot]).start()

        @pl.when(jnp.logical_not(alone))
        def _():
            send_to(src, dst, device, slot, slot)

    def order(j):
        return jnp.where(j % 2 == 0, j // 2 + 1, NZ - 1 - j // 2)

    def gather_start(buf, zslot, xslot):
        loop(0, NZ - 1, lambda j: send_to(buf.at[z, x], buf.at[z, x], z_peer(order(j)), zslot, zslot + order(j)))
        loop(1, NX, lambda e: send_to(buf.at[z, x], buf.at[z, x], x_peer(e), xslot, xslot))

    def gather_forward(buf, zslot, xslot, lo, hi):
        def step(j):
            d = order(j)
            zz = (z - d + NZ) % NZ
            landed(buf.at[zz, x], zslot + d)
            loop(1, NX, lambda e: send_to(buf.at[zz, x], buf.at[zz, x], x_peer(e), xslot, xslot + d))
        loop(lo, hi, step)

    def gather_wait(buf, xslot, g):
        for i in range(2):
            zz = 2 * g + i
            landed(buf.at[0, 0:NX - 1], xslot + (z - zz + NZ) % NZ)

    def group(i):
        return (z // 2 + jnp.where(i == 2, 3, jnp.where(i == 3, 2, i))) % 4

    def to_row(buf, slot):
        loop(1, NY, lambda d: send_to(buf.at[y, k], buf.at[y, k], y_peer(d), slot, slot))

    def to_sibling(buf, slot):
        send_to(buf.at[:, k], buf.at[:, k], sibling, slot, slot)

    def sum_core(part, cb, slot):
        send_to(part.at[:, 1 - k], cb, sibling, slot, slot)

    def sum_y(part, cb, sb, yb, slot, into):
        landed(cb, slot)
        sb[...] = part[:, k] + cb[...]
        yb[y] = sb[y]
        loop(1, NY, lambda d: send_to(sb.at[(y + d) % NY], yb.at[y], y_peer(d), into, into))

    def sum_z(src, count, came, zb, slot):
        landed(src.at[0:count - 1], came)
        zb[z] = jnp.sum(src[...], axis=0)
        loop(1, NZ, lambda d: send_to(zb.at[z], zb.at[z], z_peer(d), slot + 2, slot + 2))

    def sum_x(src, count, came, xb, slot):
        landed(src.at[0:count - 1], came)
        xb[x] = jnp.sum(src[...], axis=0)
        loop(1, NX, lambda d: send_to(xb.at[x], xb.at[x], x_peer(d), slot + 3, slot + 3))

    def sum_back_y(src, count, came, full, slot):
        landed(src.at[0:count - 1], came)
        full[y, k] = jnp.sum(src[...], axis=0)
        to_row(full, slot + 4)

    def scatter_z(part, cb, sb, zb, slot):
        landed(cb, slot)
        sb[...] = part[:, k] + cb[...]
        zb[z] = sb[z]
        loop(1, NZ, lambda d: send_to(sb.at[(z + d) % NZ], zb.at[z], z_peer(d), slot + 1, slot + 1))

    def middle_y(src, count, came, yb, slot):
        landed(src.at[0:count - 1], came)
        yb[y] = jnp.sum(src[...], axis=0)
        loop(1, NY, lambda d: send_to(yb.at[y], yb.at[y], y_peer(d), slot + 2, slot + 2))

    def back_z(src, count, came, full, slot):
        landed(src.at[0:count - 1], came)
        full[z, k] = jnp.sum(src[...], axis=0)
        loop(1, NZ, lambda d: send_to(full.at[z, k], full.at[z, k], z_peer(d), slot + 4, slot + 4))

    def sum_back_core(full, slot):
        landed(full.at[0:NY - 1, 0], slot + 4)
        to_sibling(full, slot + 5)

    def sum_end(full, slot):
        landed(full.at[:, 0], slot + 5)

    def turn(g):
        at_hi[g], at_lo[g] = split(a_v[pl.ds(2 * g, 2)].reshape(256, 512).T)

    sum_core(gpart, gcb, G_SUM)
    gather_start(pr, P_Z, P_X)
    perm(pv, pc.at[r2 // 2, r2 % 2], (r2, c2), P_PERM)
    a_copy.wait()
    turn(0)
    gather_forward(pr, P_Z, P_X, 0, 2)
    sum_y(gpart, gcb, gs, gyb, G_SUM, G_SUM + 1)
    gather_forward(pr, P_Z, P_X, 2, 4)
    landed(pc.at[0, 0], P_PERM)
    to_row(pc, P_Y)
    gather_forward(pr, P_Z, P_X, 4, 7)
    sum_z(gyb, NY, G_SUM + 1, gzb, G_SUM)
    turn(1)
    loop(2, 4, turn)
    landed(pc.at[0:NY - 1, 0], P_Y)
    to_sibling(pc, P_CORE)

    def share(i):
        g = group(i)
        gather_wait(pr, P_X, g)
        panel = split(pr[pl.ds(2 * g, 2)].reshape(256, B))

        def half(h):
            rows = pl.ds(pl.multiple_of(h * 256, 256), 256)
            part = three((at_hi[g, rows, :], at_lo[g, rows, :]), panel).reshape(4, 2, H, B)
            place = pl.ds(h * 4, 4)

            @pl.when(i == 0)
            def _():
                zpart[place] = part

            @pl.when(i > 0)
            def _():
                zpart[place] = zpart[place] + part
        loop(0, 2, half)
    sum_x(gzb, NZ, G_SUM + 2, gxb, G_SUM)
    loop(0, 4, share)
    send_to(zpart.at[:, 1 - k], zcb, sibling, Z_CORE, Z_CORE)
    sum_back_y(gxb, NX, G_SUM + 3, gf, G_SUM)
    landed(pc.at[:, 0], P_CORE)
    pct[...] = pc[...].reshape(NR * H, B).T
    sum_y(zpart, zcb, zs, zyb, Z_CORE, Z_Y)
    mpart[...] = nn(pct[...], zpart[...].reshape(NR * H, B)).reshape(NY, 2, G16, B)
    sum_core(mpart, mcb, M_SUM)
    sum_back_core(gf, G_SUM)
    scatter_z(mpart, mcb, ms, mzb, M_SUM)

    lane = lax.broadcasted_iota(jnp.int32, (128, 128), 1)
    subl = lax.broadcasted_iota(jnp.int32, (128, 128), 0)
    lane1 = lane[0:1]
    subl1 = subl[:, 0:1]

    def pair(p, q, s):
        ip = 1.0 / p
        t = q * ip
        i11 = 1.0 / (s - q * t)
        i01 = -t * i11
        return ip - t * i01, i01, i11

    def sweep(lo, hi):
        def step(i):
            j = 4 * i
            a = blk[...]
            rows = [blk[pl.ds(j + u, 1), :] for u in range(4)]
            cols = [jnp.sum(jnp.where(lane == j + u, a, 0.0), axis=1, keepdims=True) for u in range(4)]

            def at(u, v):
                return jnp.sum(jnp.where(lane1 == j + v, rows[u], 0.0), axis=1, keepdims=True)
            e00, e01, e11 = pair(at(0, 0), at(0, 1), at(1, 1))
            f00, f01, f10, f11 = at(0, 2), at(0, 3), at(1, 2), at(1, 3)
            t00, t01 = e00 * f00 + e01 * f10, e00 * f01 + e01 * f11
            t10, t11 = e01 * f00 + e11 * f10, e01 * f01 + e11 * f11
            g00, g01, g11 = pair(at(2, 2) - f00 * t00 - f10 * t10, at(2, 3) - f00 * t01 - f10 * t11,
                                 at(3, 3) - f01 * t01 - f11 * t11)
            b00, b01 = -(t00 * g00 + t01 * g01), -(t00 * g01 + t01 * g11)
            b10, b11 = -(t10 * g00 + t11 * g01), -(t10 * g01 + t11 * g11)
            a00, a01 = e00 - b00 * t00 - b01 * t01, e01 - b00 * t10 - b01 * t11
            a11 = e11 - b10 * t10 - b11 * t11
            inverse = ((a00, a01, b00, b01), (a01, a11, b10, b11), (b00, b10, g00, g01), (b01, b11, g01, g11))
            in_lane = (lane >= j) & (lane < j + 4)
            in_subl = (subl >= j) & (subl < j + 4)
            rows = [jnp.where(lane1 == j + u, -1.0, jnp.where(in_lane[0:1], 0.0, rows[u])) for u in range(4)]
            cols = [jnp.where(subl1 == j + u, -1.0, jnp.where((subl1 >= j) & (subl1 < j + 4), 0.0, cols[u]))
                    for u in range(4)]
            new = jnp.where(in_lane | in_subl, 0.0, a)
            for u in range(4):
                m = inverse[u]
                new -= cols[u] * (m[0] * rows[0] + m[1] * rows[1] + m[2] * rows[2] + m[3] * rows[3])
            blk[...] = new
        loop(lo, hi, step)

    sum_end(gf, G_SUM)
    w[...] = gf[...].reshape(B, B)
    blk[...] = w[0:128, 0:128]
    sweep(0, 10)
    landed(zyb.at[0:NY - 1], Z_Y)
    zc[y, k] = jnp.sum(zyb[...], axis=0)
    perm(zc.at[y, k], zr.at[c1 // NX, c1 % NX], (r1, c1), Z_PERM)
    sum_x(mzb, NZ, M_SUM + 1, mxb, M_SUM)
    sweep(10, 20)
    middle_y(mxb, NX, M_SUM + 3, myb, M_SUM)
    to_row(zc, ZC_Y)
    sweep(20, 32)
    landed(zr.at[0, 0], Z_PERM)
    gather_start(zr, Z_Z, Z_X)
    sub[...] = nn(w[128:256, 0:128], -blk[...])
    w[0:128, 0:128] = -blk[...]
    blk[...] = w[128:256, 128:256] - nt(sub[...], w[128:256, 0:128])
    sweep(0, 7)
    gather_forward(zr, Z_Z, Z_X, 0, 2)
    back_z(myb, NY, M_SUM + 2, mf, M_SUM)
    gather_forward(zr, Z_Z, Z_X, 2, 4)
    landed(zc.at[0:NY - 1, 0], ZC_Y)
    to_sibling(zc, ZC_CORE)
    gather_forward(zr, Z_Z, Z_X, 4, 7)
    sweep(7, 24)
    sum_back_core(mf, M_SUM)
    sweep(24, 32)
    low = nn(blk[...], sub[...])
    w[128:256, 128:256] = -blk[...]
    w[128:256, 0:128] = low
    w[0:128, 128:256] = low.T
    w[0:128, 0:128] = w[0:128, 0:128] - tn(sub[...], low)
    yc[...] = nt(w[...], pc[...].reshape(NR * H, B))
    yh[...], yl[...] = split(yc[...])
    sum_end(mf, M_SUM)
    rest = nn(mf[...].reshape(B, B), yc[...])
    landed(zc.at[:, 0], ZC_CORE)
    xc[...] = nt(w[...], zc[...].reshape(NR * H, B)) - nn(w[...], rest)
    xh[...], xl[...] = split(xc[...])

    def out_copy(g):
        place = pl.ds(2 * g, 2)
        return pltpu.make_async_copy(o_v.at[place], out_hbm.at[place], local.at[g])

    def update(i):
        g = group(i)
        gather_wait(zr, Z_X, g)
        place = pl.ds(2 * g, 2)
        change = three(split(pr[place].reshape(256, B)), (xh[...], xl[...]))
        change += three(split(zr[place].reshape(256, B)), (yh[...], yl[...]))
        rows = r * 1024 + g * 256 + lax.broadcasted_iota(jnp.int32, (256, 512), 0)
        cols = c * 512 + lax.broadcasted_iota(jnp.int32, (256, 512), 1)
        old = a_v[place].reshape(256, 512)
        o_v[place] = jnp.where(rows >= cols, old - change, old).reshape(2, NX, H, 512)
        out_copy(g).start()
    loop(0, 4, update)

    for slot in (P_Z, Z_Z):
        left(pr.at[0:NZ - 1, 0], slot)
    for slot in (P_X, Z_X):
        left(pr.at[:, 0:NX - 1], slot)
    for slot in (P_Y, Z_Y, ZC_Y):
        left(pc.at[0:NY - 1, 0], slot)
    for slot in (P_CORE, Z_CORE, ZC_CORE):
        left(pc.at[:, 0], slot)
    for slot in (G_SUM, M_SUM):
        left(gf.at[:, 0], slot)
        left(gf.at[0:NY - 1, 0], slot + 1)
        left(gf.at[0:NZ - 1, 0], slot + 2)
        left(gf.at[0:NX - 1, 0], slot + 3)
        left(gf.at[0:NY - 1, 0], slot + 4)
        left(gf.at[:, 0], slot + 5)

    @pl.when(jnp.logical_not(alone))
    def _():
        left(pc.at[0, 0], P_PERM)
        left(pc.at[0, 0], Z_PERM)

    loop(0, 4, lambda g: out_copy(g).wait())


def on_device(matrix, panel):
    vm = lambda *s: pltpu.VMEM(s, F32)
    bf = lambda *s: pltpu.VMEM(s, jnp.bfloat16)
    sums = [vm(NY, 2, G16, B), vm(NY, G16, B), vm(NY, G16, B), vm(NY, G16, B), vm(NZ, G16, B), vm(NX, G16, B),
            vm(NY, 2, G16, B)]
    out = pl.pallas_call(
        kernel,
        out_shape=jax.ShapeDtypeStruct((NZ, NX, H, 512), F32),
        in_specs=[pl.BlockSpec(memory_space=pltpu.HBM), pl.BlockSpec(memory_space=pltpu.HBM)],
        out_specs=pl.BlockSpec(memory_space=pltpu.HBM),
        scratch_shapes=[
            vm(NZ, NX, H, 512), bf(4, 512, 256), bf(4, 512, 256), vm(NZ, NX, H, 512), vm(H, B),
            vm(NZ, NX, H, B), vm(NZ, NX, H, B), vm(NY, 2, H, B), vm(B, NR * H), vm(NY, 2, H, B),
            vm(NY, 2, H, B), vm(NY, H, B), vm(NY, H, B), vm(NY, H, B),
            *sums, *sums,
            vm(B, B), vm(128, 128), vm(128, 128), vm(B, 512), bf(B, 512), bf(B, 512), vm(B, 512), bf(B, 512), bf(B, 512),
            pltpu.SemaphoreType.DMA((SEMS,)), pltpu.SemaphoreType.DMA((SEMS,)), pltpu.SemaphoreType.DMA((5,)),
        ],
        compiler_params=pltpu.CompilerParams(
            collective_id=0, has_side_effects=True, vmem_limit_bytes=50 * 1024 * 1024),
        cost_estimate=pl.CostEstimate(flops=8 * 10**9, bytes_accessed=8 * 2**20, transcendentals=0),
    )(matrix.reshape(NZ, NX, H, 512), panel)
    return out.reshape(1024, 512)


def solution(mesh):
    return jax.shard_map(
        on_device,
        mesh=mesh,
        in_specs=(P("row", "col"), P(("row", "col"), None)),
        out_specs=P("row", "col"),
        check_vma=False,
    )
```
